256 devices in a mesh: ctx: 32 (over x, z), tp: 8 (over y, core).
Axes of the slice: x: 4, y: 4, z: 8, core: 2. Of those that a mesh axis runs over, the one named last changes fastest.
Arguments:
- queries: bfloat16 [4096, 8192], P('ctx', 'tp'), may hold values from -160 to 160
- key_rows: bfloat16 [4096, 1024], P('ctx', 'tp'), may hold values from -4.5 to 4.5
- value_rows: bfloat16 [4096, 1024], P('ctx', 'tp'), may hold values from -6 to 6
- doc_lengths: int32 [16], replicated, may hold values from 1 to 2112, 4096 in all
- gate_input: bfloat16 [4096, 8192], P('ctx', 'tp'), may hold values from -6 to 6
- bc_input: bfloat16 [4096, 2, 4, 256], P('ctx'), may hold values from -1.796875 to 1.796875
- step_size: float32 [4096, 128], P('ctx', 'tp'), may hold values from 0.5 to 2
- decay_rate: float32 [128], P('tp'), may hold values from 0 to 1, as said below
- skip_gain: float32 [128], P('tp'), may hold values from 1 to 4
- conv_x: float32 [4, 8192], P(None, 'tp'), may hold values from -3 to 3
- conv_bc: float32 [4, 2, 4, 256], replicated, may hold values from -3 to 3
- norm_gain: float32 [8192], P('tp'), may hold values from 0.1 to 1.9
Outputs:
- mixed: bfloat16 [4096, 8192], P('ctx', 'tp')
The draws below stay inside these ranges and needn't reach their ends.
Inputs may be any that keep to these rules, and one draw needn't show every extreme that they name: `doc_lengths`: documents lie end to end in token order; the longest has exactly 2112 tokens. `decay_rate`: positive rates.
All inputs are finite; a program needn't handle non-finite values.
Results may differ from the reference program's by a relative error of at most 0.02.
Values may be sent and summed in bfloat16 or wider, within the bound.
No kernel may reach another device: no remote copies, remote signals or barrier semaphores. Data moves between devices by JAX's collectives and lax.ppermute only.
A program may use at most 128 MiB of HBM per device.

```python
import math
import jax
import jax.numpy as jnp
import numpy as np
from jax import lax

HD = 128
HQ_DEV = 8
MH_DEV = 16
P_SIZE = 64
N = 256
KW = 4
TOKENS = 4096
H = 64
KVH = 8
MH = 128
NG = 4
MOST = 2112
NDOC = 16


def base_keys(key):
    return jnp.clip(jax.random.normal(key, (TOKENS, KVH * HD), jnp.float32), -4.5, 4.5)


def draw_key_rows(key, part):
    base = base_keys(key)
    return base.astype(jnp.bfloat16)


def draw_queries(key, part):
    key = jax.random.fold_in(key, 5)
    own_key = jax.random.fold_in(key, 0)
    drawn = jnp.clip(jax.random.normal(own_key, (TOKENS, H * HD), jnp.float32), -4.5, 4.5)
    return drawn.astype(jnp.bfloat16)


def draw_decay_rate(key, part):
    key = jax.random.fold_in(key, 7)
    pick_key, fast_key, slow_key = jax.random.split(key, 3)
    slow_share = 0.5
    slow_heads = jax.random.uniform(pick_key, (MH,), jnp.float32) < slow_share
    fast_rate = jnp.exp(jax.random.uniform(fast_key, (MH,), jnp.float32, math.log(1.0 / 50.0), math.log(1.0 / 30.0)))
    slow_rate = jnp.exp(jax.random.uniform(slow_key, (MH,), jnp.float32, math.log(0.05 / MOST), math.log(2.0 / MOST)))
    return jnp.where(slow_heads, slow_rate, fast_rate)


def block_levels(key, dims, pieces, smallest, high):
    loudness, own = 1.0, jax.random.fold_in(key, 6)
    for dim, blocks in pieces:
        draws = jnp.exp(jax.random.uniform(jax.random.fold_in(own, dim), (blocks,), jnp.float32, smallest / len(pieces), high / len(pieces)))
        loudness = loudness * jnp.repeat(draws, dims[dim] // blocks).reshape([-1 if axis == dim else 1 for axis in range(len(dims))])
    return loudness


def profile(amount, total, limit, slope):
    loads = [(1 << 20) // math.isqrt(rank ** slope) + 1 for rank in range(2, amount + 1)]
    spare, given = total - limit - (amount - 1), [1] * (amount - 1)
    while spare > 0:
        free = [i for i in range(amount - 1) if given[i] < limit]
        mass, left = sum([loads[i] for i in free]), spare
        for i in free:
            extra = min(limit - given[i], max(1, left * loads[i] // mass), spare)
            given[i] = given[i] + extra
            spare = spare - extra
    return np.array([limit] + given)


def ragged_sizes(rng, count, total, bound, lean):
    if count == 2:
        one = jax.random.randint(rng, (), max(1, total - bound), min(bound, total - 1) + 1)
        return jnp.stack([one, total - one])
    tallies = jnp.asarray(profile(count, total, bound, lean), jnp.int32)
    pairs = (count - 1) // 2
    giver, sink = tallies[1:1 + 2 * pairs:2], tallies[2:2 + 2 * pairs:2]
    margin = jnp.minimum(giver - 1, bound - sink)
    moved = jax.random.randint(jax.random.fold_in(rng, 1), (pairs,), 0, 1 << 20) % (margin + 1)
    tallies = tallies.at[1:1 + 2 * pairs:2].set(giver - moved).at[2:2 + 2 * pairs:2].set(sink + moved)
    return tallies[jax.random.permutation(jax.random.fold_in(rng, 2), count)]


def scatter_about(rng, shape, width, most, shards=(), kind=jnp.bfloat16):
    drawn = jax.random.normal(rng, shape, jnp.float32) * width
    if len(shards) > 0:
        drawn = block_levels(rng, shape, shards, -0.22, 0.18) * drawn
    return jnp.clip(drawn, min=-most, max=most).astype(kind)


def setup_inputs(seed: int = 0) -> dict:
    key_list = jax.random.split(jax.random.key(seed), 13)
    queries = draw_queries(jax.random.fold_in(key_list[12], 71), 0)
    key_rows = draw_key_rows(jax.random.fold_in(key_list[12], 71), 0)
    value_rows = scatter_about(key_list[2], (TOKENS, KVH * HD), 1.0, 6.0, ((0, 32), (1, 8)))
    doc_lengths = ragged_sizes(key_list[3], NDOC, TOKENS, MOST, 2).astype(jnp.int32)
    gate_input = scatter_about(key_list[4], (TOKENS, MH * P_SIZE), 1.0, 6.0, ((0, 32), (1, 8)))
    bc_input = scatter_about(key_list[5], (TOKENS, 2, NG, N), 0.3, 1.796875, ((0, 32),))
    step_size = jnp.clip(jnp.exp(math.log(2.0) - 1.3862944 * jax.random.uniform(key_list[6], (TOKENS, MH), jnp.float32) ** block_levels(key_list[6], (TOKENS, MH), ((0, 32), (1, 8)), -0.2, 0.2)), 0.5, 2.0)
    decay_rate = draw_decay_rate(jax.random.fold_in(key_list[12], 71), 0)
    skip_gain = jnp.clip(1.0 + 3.0 * jax.random.uniform(key_list[8], (MH,), jnp.float32) ** block_levels(key_list[8], (MH,), ((0, 8),), -0.2, 0.2), 1.0, 4.0)
    conv_x = scatter_about(key_list[9], (KW, MH * P_SIZE), KW ** -0.5, 3.0, ((1, 8),), jnp.float32)
    conv_bc = scatter_about(key_list[10], (KW, 2, NG, N), KW ** -0.5, 3.0, (), jnp.float32)
    norm_gain = jnp.clip(1.0 + 0.18 * jax.random.normal(key_list[11], (MH * P_SIZE,), jnp.float32), 0.1, 1.9)
    return {"queries": queries, "key_rows": key_rows, "value_rows": value_rows, "doc_lengths": doc_lengths, "gate_input": gate_input, "bc_input": bc_input, "step_size": step_size, "decay_rate": decay_rate, "skip_gain": skip_gain, "conv_x": conv_x, "conv_bc": conv_bc, "norm_gain": norm_gain}


EPSILON = 1e-05

def rounded(value):
    return lax.optimization_barrier(value.astype(jnp.bfloat16))

def start_table(doc_lengths):
    doc_ends = jnp.cumsum(doc_lengths).astype(jnp.int32)
    return doc_ends - doc_lengths

def doc_start(doc_starts, positions):
    covered = doc_starts[None, :] <= positions[:, None]
    return lax.optimization_barrier(jnp.max(jnp.where(covered, doc_starts[None, :], jnp.zeros_like(doc_starts)[None, :]), axis=1))

def attention(queries, key_rows, value_rows, doc_starts):
    query_block = math.gcd(TOKENS, 128)
    key_span = min(MOST + query_block, TOKENS)
    block_count = TOKENS // query_block
    score_scale = 1.0 / math.sqrt(HD)
    query_blocks = queries.reshape(block_count, query_block, KVH, HQ_DEV, HD)

    def visit(entries):
        block_index, block = entries
        query_start = block_index * query_block
        key_start = jnp.clip(query_start + query_block - key_span, 0, TOKENS - key_span).astype(jnp.int32)
        key_slab = lax.dynamic_slice_in_dim(key_rows, key_start, key_span, 0).reshape(key_span, KVH, HD)
        value_slab = lax.dynamic_slice_in_dim(value_rows, key_start, key_span, 0).reshape(key_span, KVH, HD)
        query_pos = (query_start + jnp.arange(query_block, dtype=jnp.int32)).astype(jnp.int32)
        key_pos = (key_start + jnp.arange(key_span, dtype=jnp.int32)).astype(jnp.int32)
        first_token = doc_start(doc_starts, query_pos)
        visible = (key_pos[None, :] <= query_pos[:, None]) & (key_pos[None, :] >= first_token[:, None])
        scores = jnp.einsum('qgjd,kgd->gjqk', block.astype(jnp.float32), key_slab.astype(jnp.float32), precision=lax.Precision.HIGHEST) * score_scale
        scores = jnp.where(visible[None, None], scores, -jnp.inf)
        maximum = lax.optimization_barrier(jnp.max(scores, axis=-1, keepdims=True))
        exponent = jnp.exp(scores - maximum)
        totals = lax.optimization_barrier(jnp.sum(exponent, axis=-1))
        weights = rounded(exponent)
        summed = jnp.einsum('gjqk,kgd->qgjd', weights.astype(jnp.float32), value_slab.astype(jnp.float32), precision=lax.Precision.HIGHEST)
        output = summed / jnp.transpose(totals, (2, 0, 1))[..., None]
        return output.reshape(query_block, KVH * HQ_DEV * HD).astype(jnp.bfloat16)
    outputs = lax.map(visit, (jnp.arange(block_count, dtype=jnp.int32), query_blocks))
    return outputs.reshape(TOKENS, H * HD)

def causal_conv(inputs, taps, first_token, positions):
    padded = jnp.concatenate([jnp.zeros((KW - 1,) + inputs.shape[1:], inputs.dtype), inputs], 0)
    accumulated = jnp.zeros(inputs.shape, jnp.float32)
    for shift_by in range(KW):
        tap_rows = padded[KW - 1 - shift_by:KW - 1 - shift_by + TOKENS].astype(jnp.float32)
        usable = (positions - shift_by >= first_token).reshape((TOKENS,) + (1,) * (inputs.ndim - 1))
        accumulated = accumulated + jnp.where(usable, tap_rows * taps[KW - 1 - shift_by], 0.0)
    return accumulated

def scan_layer(mixed_input, bc_conv, step_size, decay_rate, skip_gain, first_token):
    block_size = math.gcd(TOKENS, 256)
    block_count = TOKENS // block_size
    group_heads = 2 * MH_DEV
    input_blocks = mixed_input.reshape(block_count, block_size, MH, P_SIZE)
    bc_blocks = bc_conv.reshape(block_count, block_size, 2, NG, N)
    step_blocks = step_size.reshape(block_count, block_size, MH)
    start_blocks = first_token.reshape(block_count, block_size)
    highest = lax.Precision.HIGHEST

    def visit(state, entries):
        block_index, input_part, bc_part, step_part, start_part = entries
        block_start = block_index * block_size
        positions = (block_start + jnp.arange(block_size, dtype=jnp.int32)).astype(jnp.int32)
        log_decay = -decay_rate[None, :] * step_part
        cumulated = jnp.cumsum(log_decay, axis=0)
        b_values = bc_part[:, 0].astype(jnp.float32)
        c_values = bc_part[:, 1].astype(jnp.float32)
        gram_matrix = jnp.einsum('tgn,sgn->gts', c_values, b_values, precision=highest)
        gram_heads = jnp.repeat(gram_matrix, group_heads, axis=0)
        visible = (positions[None, :] >= start_part[:, None]) & (positions[None, :] <= positions[:, None])
        cum_heads = cumulated.T
        log_gap = jnp.where(visible[None], cum_heads[:, :, None] - cum_heads[:, None, :], -jnp.inf)
        mixing = gram_heads * jnp.exp(log_gap) * step_part.T[:, None, :]
        input_wide = input_part.astype(jnp.float32)
        inner_part = jnp.einsum('hts,shp->thp', mixing, input_wide, precision=highest)
        carry_in = (start_part < block_start).astype(jnp.float32)
        c_heads = jnp.repeat(c_values, group_heads, axis=1)
        carried_part = jnp.einsum('thn,hpn->thp', c_heads, state, precision=highest)
        carried_part = carried_part * (jnp.exp(cumulated) * carry_in[:, None])[:, :, None]
        output = inner_part + carried_part + skip_gain[None, :, None] * input_wide
        last_start = start_part[-1]
        state_weight = jnp.where((positions >= last_start)[:, None], jnp.exp(cumulated[-1][None, :] - cumulated), 0.0)
        state_weight = state_weight * step_part
        b_heads = jnp.repeat(b_values, group_heads, axis=1)
        block_state = jnp.einsum('shp,shn->hpn', state_weight[:, :, None] * input_wide, b_heads, precision=highest)
        carry_decay = jnp.where(last_start < block_start, jnp.exp(cumulated[-1]), 0.0)
        state = carry_decay[:, None, None] * state + block_state
        return (state, output)
    initial = jnp.zeros((MH, P_SIZE, N), jnp.float32)
    _, outputs = lax.scan(visit, initial, (jnp.arange(block_count, dtype=jnp.int32), input_blocks, bc_blocks, step_blocks, start_blocks))
    return outputs.reshape(TOKENS, MH * P_SIZE)

def reference(queries, key_rows, value_rows, doc_lengths, gate_input, bc_input, step_size, decay_rate, skip_gain, conv_x, conv_bc, norm_gain):
    doc_starts = start_table(doc_lengths)
    positions = jnp.arange(TOKENS, dtype=jnp.int32)
    first_token = doc_start(doc_starts, positions)
    attended = rounded(attention(queries, key_rows, value_rows, doc_starts))
    mixed_input = rounded(jax.nn.silu(causal_conv(attended, conv_x, first_token, positions)))
    bc_conv = rounded(jax.nn.silu(causal_conv(bc_input, conv_bc, first_token, positions)))
    ssm_out = scan_layer(mixed_input, bc_conv, step_size, decay_rate, skip_gain, first_token)
    gated = ssm_out * jax.nn.silu(gate_input.astype(jnp.float32))
    grouped = gated.reshape(TOKENS, NG, 2 * MH_DEV * P_SIZE)
    mean_square = lax.optimization_barrier(jnp.mean(grouped * grouped, axis=-1, keepdims=True))
    normalized = grouped * lax.rsqrt(mean_square + EPSILON)
    return (normalized.reshape(TOKENS, MH * P_SIZE) * norm_gain[None, :]).astype(jnp.bfloat16)
```

```python
import math

import jax
import jax.numpy as jnp
from jax import lax
from jax.experimental import pallas as pl
from jax.experimental.pallas import tpu as pltpu
from jax.sharding import PartitionSpec as P

EPSILON = 1e-05
NEGATIVE_FILL = -1e30
NEAR = 8
FAR = 4
SHARD = 128
ROW = NEAR * SHARD
CHUNK = 256
CHUNKS = ROW // CHUNK
HEAD = 128
STATE = 256
RIM = 16
PAST = 9 * CHUNK
QUERY_ROWS = SHARD + 16
PACK_ROWS = QUERY_ROWS + 2 * SHARD
EXP2_SCALE = math.log2(math.e) / math.sqrt(HEAD)
F32 = jnp.float32
BF16 = jnp.bfloat16


def near_groups():
    return [[x * NEAR + z for z in range(NEAR)] for x in range(FAR)]


def exchange_near(x):
    return lax.all_to_all(x, "ctx", 0, 0, axis_index_groups=near_groups(), tiled=True)


def from_row_behind(x, by):
    pairs = [(x0 * NEAR + z, (x0 + by) * NEAR + z) for x0 in range(FAR - by) for z in range(NEAR)]
    return lax.ppermute(x, "ctx", pairs)


def from_shard_behind(x):
    return lax.ppermute(x, "ctx", [(i, i + 1) for i in range(NEAR * FAR - 1)])


def with_partner(x):
    count = lax.axis_size("tp")
    return lax.ppermute(x, "tp", [(t, t ^ 1) for t in range(count)])


def first_tokens(docs, pos):
    begin = jnp.int32(0)
    first = pos
    for d in range(docs.shape[0]):
        first = jnp.where(pos >= begin, begin, first)
        begin = begin + docs[d]
    return first


def columns_of(rows):
    count = rows[0].shape[1]
    rows = list(rows) + [jnp.zeros((1, count), F32)] * (8 - len(rows))
    return jnp.transpose(jnp.concatenate(rows, 0))


def silu(v):
    return v / (1.0 + jnp.exp(-v))


def pair_kernel(keys, values, out):
    for n in range(NEAR):
        out[n, :, 0:HEAD] = keys[...]
        out[n, :, HEAD:] = values[...]


def pack_kernel(info, docs, queries, steps, raw, rim, taps, out, ext):
    ext[0:RIM] = rim[...].astype(F32)
    ext[RIM:] = raw[...].astype(F32)
    pos = info[3] + lax.broadcasted_iota(jnp.int32, (1, SHARD), 1)
    since = columns_of([(pos - first_tokens(docs, pos)).astype(F32)])[:, 0:1]
    acc = jnp.zeros((SHARD, STATE), F32)
    for m in range(4):
        part = ext[RIM - m : RIM - m + SHARD] * taps[3 - m : 4 - m]
        acc = acc + jnp.where(since >= m, part, 0.0)
    convolved = silu(acc).astype(BF16)
    wide = jnp.concatenate([steps[...], jnp.zeros((SHARD, HEAD - 2 * NEAR), F32)], 1)
    rows = jnp.transpose(wide)
    high = rows.astype(BF16).astype(F32)
    middle = (rows - high).astype(BF16).astype(F32)
    low = rows - high - middle
    for n in range(NEAR):
        out[n, 0:SHARD] = queries[:, n * HEAD : (n + 1) * HEAD]
        two = slice(2 * n, 2 * n + 2)
        out[n, SHARD:QUERY_ROWS] = jnp.concatenate(
            [high[two], middle[two], low[two], jnp.zeros((10, HEAD), F32)], 0
        ).astype(BF16)
        out[n, QUERY_ROWS : QUERY_ROWS + SHARD] = convolved[:, 0:HEAD]
        out[n, QUERY_ROWS + SHARD :] = convolved[:, HEAD:]


def two_heads(first, second, shape):
    lane = lax.broadcasted_iota(jnp.int32, shape, 1)
    return jnp.where(lane < HEAD // 2, jnp.broadcast_to(first, shape), jnp.broadcast_to(second, shape))


def mixing_kernel(
    info, docs, rates, received, other, mix, b_t, c_out, weigh, enter, enter_row, decays
):
    core_zero = info[2] == 0
    near = info[1]
    for s in range(NEAR):
        rows = slice(s * SHARD, (s + 1) * SHARD)
        for half in range(2):
            columns = slice(half * HEAD, (half + 1) * HEAD)
            at = slice(QUERY_ROWS + half * SHARD, QUERY_ROWS + (half + 1) * SHARD)
            from_other = slice(half * SHARD, (half + 1) * SHARD)
            mine, theirs = received[s, at], other[s, from_other]
            b_values = jnp.where(core_zero, mine, theirs)
            c_out[rows, columns] = jnp.where(core_zero, theirs, mine)
            b_t[columns, rows] = jnp.transpose(b_values.astype(F32)).astype(BF16)
    pieces = []
    for s in range(NEAR):
        piece = received[s, SHARD : SHARD + 16, :].astype(F32)
        pieces.append(piece[0:2] + piece[2:4] + piece[4:6])
    steps = jnp.concatenate(pieces, 1)
    rate = jnp.concatenate(
        [jnp.full((1, ROW), rates[2 * near], F32), jnp.full((1, ROW), rates[2 * near + 1], F32)], 0
    )
    log_decay = jnp.concatenate([-rate * steps, jnp.zeros((6, ROW), F32)], 0)
    row_start = info[0]
    pos = row_start + lax.broadcasted_iota(jnp.int32, (1, ROW), 1)
    first = first_tokens(docs, pos)
    below = lax.broadcasted_iota(jnp.int32, (CHUNK, CHUNK), 0)
    across = lax.broadcasted_iota(jnp.int32, (CHUNK, CHUNK), 1)
    upper = jnp.where(below <= across, 1.0, 0.0).astype(F32)
    before = jnp.zeros((2, 1), F32)
    decay_rows = []
    for k in range(CHUNKS):
        rows = slice(k * CHUNK, (k + 1) * CHUNK)
        chunk_start = row_start + k * CHUNK
        local = jnp.dot(
            log_decay[:, rows],
            upper,
            precision=lax.Precision.HIGHEST,
            preferred_element_type=F32,
        )[0:2]
        total = local[:, CHUNK - 1 : CHUNK]
        last_start = first[:, (k + 1) * CHUNK - 1 : (k + 1) * CHUNK]
        w = jnp.where(pos[:, rows] >= last_start, jnp.exp(total - local), 0.0) * steps[:, rows]
        e_chunk = jnp.where(first[:, rows] < chunk_start, jnp.exp(local), 0.0)
        e_row = jnp.where(first[:, rows] < row_start, jnp.exp(before + local), 0.0)
        crossing = jnp.where(last_start < chunk_start, jnp.exp(total), 0.0)
        decay_rows.append(two_heads(crossing[0:1], crossing[1:2], (1, HEAD)))
        before = before + total
        columns = jnp.transpose(jnp.concatenate([w, e_chunk, e_row, local], 0))
        since = columns_of([(first[:, rows] - chunk_start).astype(F32)])[:, 0:1]
        shape = (CHUNK, HEAD)
        weigh[rows] = two_heads(columns[:, 0:1], columns[:, 1:2], shape)
        enter[rows] = two_heads(columns[:, 2:3], columns[:, 3:4], shape)
        enter_row[rows] = two_heads(columns[:, 4:5], columns[:, 5:6], shape)
        gram = jnp.dot(c_out[rows], b_t[:, rows], preferred_element_type=F32)
        visible = (across <= below) & (across.astype(F32) >= since)
        for h in range(2):
            gap = jnp.where(visible, columns[:, 6 + h : 7 + h] - local[h : h + 1], NEGATIVE_FILL)
            mix[k, h] = (gram * jnp.exp(gap) * steps[h : h + 1, rows]).astype(BF16)
    last = jnp.where(first[:, ROW - 1 : ROW] < row_start, jnp.exp(before), 0.0)
    decay_rows.append(two_heads(last[0:1], last[1:2], (1, HEAD)))
    decays[...] = jnp.concatenate(decay_rows + [jnp.zeros((3, HEAD), F32)], 0)


def attend_kernel(
    info,
    docs,
    received,
    halo,
    own,
    back1,
    back2,
    back3,
    taps,
    b_t,
    weigh,
    decays,
    x_out,
    states,
    handed,
    keys,
    seen,
    top,
    total,
    summed,
    halo_seen,
    halo_top,
    halo_total,
    halo_summed,
    ext,
    sems,
):
    copies = [
        pltpu.make_async_copy(own, keys.at[pl.ds(PAST, ROW)], sems.at[0]),
        pltpu.make_async_copy(back1, keys.at[pl.ds(PAST - ROW, ROW)], sems.at[1]),
        pltpu.make_async_copy(back2, keys.at[pl.ds(PAST - 2 * ROW, ROW)], sems.at[2]),
        pltpu.make_async_copy(back3, keys.at[pl.ds(0, CHUNK)], sems.at[3]),
    ]
    for copy in copies:
        copy.start()
    row_start = info[0]
    near = info[1]
    pos = row_start + lax.broadcasted_iota(jnp.int32, (1, ROW), 1)
    first = first_tokens(docs, pos)
    columns = columns_of([(first - row_start).astype(F32), (pos - first).astype(F32)])
    since = columns[:, 1:2]
    seen[...] = jnp.broadcast_to(columns[:, 0:1], (ROW, HEAD))
    halo_pos = row_start - RIM + lax.broadcasted_iota(jnp.int32, (1, HEAD), 1)
    halo_first = columns_of([(first_tokens(docs, halo_pos) - row_start).astype(F32)])
    halo_seen[...] = jnp.broadcast_to(halo_first[0:RIM, 0:1], (RIM, HEAD))
    begin = jnp.int32(0)
    cross_start, cross_end = jnp.int32(0), jnp.int32(0)
    for d in range(docs.shape[0]):
        inside = begin <= row_start
        cross_start = jnp.where(inside, begin, cross_start)
        begin = begin + docs[d]
        cross_end = jnp.where(inside, begin, cross_end)
    lowest = lax.div(cross_start - row_start + PAST, jnp.int32(CHUNK))
    reached = cross_end - row_start

    def scores_of(query, block, seen_rows, causal):
        at = pl.ds(pl.multiple_of(block * CHUNK, CHUNK), CHUNK)
        raw = lax.dot_general(
            query, keys[at, 0:HEAD], (((1,), (1,)), ((), ())), preferred_element_type=F32
        )
        halves = []
        for half in range(2):
            offset = block * CHUNK - PAST + half * HEAD
            place = lax.broadcasted_iota(jnp.int32, (1, HEAD), 1) + offset
            visible = place.astype(F32) >= seen_rows
            if causal is not None:
                down = lax.broadcasted_iota(jnp.int32, (query.shape[0], HEAD), 0) + causal
                along = lax.broadcasted_iota(jnp.int32, (query.shape[0], HEAD), 1) + half * HEAD
                visible = visible & (along <= down)
            part = raw[:, half * HEAD : (half + 1) * HEAD]
            halves.append(jnp.where(visible, part, NEGATIVE_FILL))
        return halves, keys[at, HEAD:]

    def fold(query, block, seen_ref, top_ref, total_ref, summed_ref, rows, causal, fresh):
        (left, right), values = scores_of(query, block, seen_ref[rows], causal)
        largest = jnp.max(jnp.maximum(left, right), axis=1, keepdims=True)
        if fresh:
            new_top = jnp.broadcast_to(largest, left.shape)
        else:
            old_top = top_ref[rows]
            new_top = jnp.maximum(old_top, largest)
            factor = jnp.exp2((old_top - new_top) * EXP2_SCALE)
        left = jnp.exp2((left - new_top) * EXP2_SCALE)
        right = jnp.exp2((right - new_top) * EXP2_SCALE)
        weights = jnp.concatenate([left.astype(BF16), right.astype(BF16)], 1)
        product = jnp.dot(weights, values, preferred_element_type=F32)
        top_ref[rows] = new_top
        if fresh:
            total_ref[rows] = left + right
            summed_ref[rows] = product
        else:
            total_ref[rows] = total_ref[rows] * factor + (left + right)
            summed_ref[rows] = summed_ref[rows] * factor + product

    def query_of(i):
        return received[2 * i : 2 * i + 2, 0:SHARD, :].reshape(CHUNK, HEAD)

    def fold_row(i, block, causal, fresh):
        fold(
            query_of(i),
            block,
            seen,
            top,
            total,
            summed,
            slice(i * CHUNK, (i + 1) * CHUNK),
            causal,
            fresh,
        )

    def fold_halo(block, causal, fresh):
        fold(
            halo[...],
            block,
            halo_seen,
            halo_top,
            halo_total,
            halo_summed,
            slice(0, RIM),
            causal,
            fresh,
        )

    for copy in copies:
        copy.wait()
    own_block = PAST // CHUNK
    fold_halo(own_block - 1, CHUNK - RIM, True)
    for back in range(CHUNKS):
        for i in range(back, CHUNKS):
            fold_row(i, own_block + i - back, 0 if back == 0 else None, back == 0)

    def earlier(count):
        def visit(n, carry):
            block = own_block - 1 - n
            for i in range(count):
                fold_row(i, block, None, False)

            @pl.when(n > 0)
            def _():
                fold_halo(block, None, False)

            return carry

        lax.fori_loop(0, own_block - lowest, visit, 0)

    @pl.when(reached <= CHUNK)
    def _():
        earlier(1)

    @pl.when((reached > CHUNK) & (reached <= 2 * CHUNK))
    def _():
        earlier(2)

    @pl.when(reached > 2 * CHUNK)
    def _():
        earlier(CHUNKS)

    def finish(total_ref, summed_ref):
        whole = jnp.sum(total_ref[...], axis=1, keepdims=True)
        return (summed_ref[...] / whole).astype(BF16).astype(F32)

    ext[0:RIM] = finish(halo_total, halo_summed)
    ext[RIM:] = finish(total, summed)
    own_taps = taps[:, pl.ds(pl.multiple_of(near * HEAD, HEAD), HEAD)]
    state = jnp.zeros((STATE, HEAD), F32)
    for k in range(CHUNKS):
        rows = slice(k * CHUNK, (k + 1) * CHUNK)
        acc = jnp.zeros((CHUNK, HEAD), F32)
        for m in range(4):
            part = ext[RIM - m + k * CHUNK : RIM - m + (k + 1) * CHUNK] * own_taps[3 - m : 4 - m]
            acc = acc + jnp.where(since[rows] >= m, part, 0.0)
        x = silu(acc).astype(BF16)
        x_out[rows] = x
        states[k] = state.astype(BF16)
        weighed = (x.astype(F32) * weigh[rows]).astype(BF16)
        state = state * decays[k : k + 1] + jnp.dot(
            b_t[:, rows], weighed, preferred_element_type=F32
        )
    handed[0:STATE] = state.astype(BF16)
    decay = decays[CHUNKS : CHUNKS + 1]
    high = decay.astype(BF16).astype(F32)
    handed[STATE:] = jnp.concatenate(
        [high, decay - high, jnp.zeros((14, HEAD), F32)], 0
    ).astype(BF16)


def inner_kernel(info, skip, mix, x_in, c_in, states, enter, y_out):
    near = info[1]
    gain = two_heads(skip[2 * near], skip[2 * near + 1], (1, HEAD))
    lane = lax.broadcasted_iota(jnp.int32, (CHUNK, HEAD), 1)
    for k in range(CHUNKS):
        rows = slice(k * CHUNK, (k + 1) * CHUNK)
        x = x_in[rows]
        left = jnp.dot(mix[k, 0], x, preferred_element_type=F32)
        right = jnp.dot(mix[k, 1], x, preferred_element_type=F32)
        y = jnp.where(lane < HEAD // 2, left, right) + x.astype(F32) * gain
        if k > 0:
            y = y + enter[rows] * jnp.dot(c_in[rows], states[k], preferred_element_type=F32)
        y_out[rows] = y


def carried_kernel(y_in, enter_row, c_in, back1, back2, back3, y_out):
    def parts(ref):
        tail = ref[STATE:].astype(F32)
        return ref[0:STATE].astype(F32), tail[0:1] + tail[1:2]

    state1, decay1 = parts(back1)
    state2, decay2 = parts(back2)
    state3, _ = parts(back3)
    entering = (state1 + decay1 * (state2 + decay2 * state3)).astype(BF16)
    for k in range(CHUNKS):
        rows = slice(k * CHUNK, (k + 1) * CHUNK)
        carried = jnp.dot(c_in[rows], entering, preferred_element_type=F32)
        y_out[rows] = (y_in[rows] + enter_row[rows] * carried).astype(BF16)


def gated_of(y, gate, h):
    return y[h].astype(F32) * silu(gate[:, h * HEAD : (h + 1) * HEAD].astype(F32))


def square_kernel(y, gate, sums):
    acc = jnp.zeros((SHARD, HEAD), F32)
    for h in range(NEAR):
        gated = gated_of(y, gate, h)
        acc = acc + gated * gated
    sums[...] = jnp.broadcast_to(jnp.sum(acc, axis=1, keepdims=True), (SHARD, HEAD))


def norm_kernel(y, gate, sums, partner, gain, out):
    mean = (sums[...] + partner[...]) / (2.0 * NEAR * HEAD)
    scale = lax.rsqrt(mean + EPSILON)
    for h in range(NEAR):
        columns = slice(h * HEAD, (h + 1) * HEAD)
        out[:, columns] = (gated_of(y, gate, h) * scale * gain[:, columns]).astype(BF16)


def call(kernel, outs, args, smem=0, raw=(), scratch=(), flops=0, mib=48):
    specs = []
    for n in range(len(args)):
        if n < smem:
            specs.append(pl.BlockSpec(memory_space=pltpu.SMEM))
        elif n in raw:
            specs.append(pl.BlockSpec(memory_space=pl.ANY))
        else:
            specs.append(pl.BlockSpec(memory_space=pltpu.VMEM))
    single = len(outs) == 1
    shapes = [jax.ShapeDtypeStruct(shape, kind) for shape, kind in outs]
    out_specs = [pl.BlockSpec(memory_space=pltpu.VMEM)] * len(outs)
    return pl.pallas_call(
        kernel,
        out_shape=shapes[0] if single else shapes,
        in_specs=specs,
        out_specs=out_specs[0] if single else out_specs,
        scratch_shapes=list(scratch),
        compiler_params=pltpu.CompilerParams(vmem_limit_bytes=mib * 1024 * 1024),
        cost_estimate=pl.CostEstimate(flops=flops, bytes_accessed=1 << 21, transcendentals=0),
    )(*args)


def on_device(
    queries,
    key_rows,
    value_rows,
    doc_lengths,
    gate_input,
    bc_input,
    step_size,
    decay_rate,
    skip_gain,
    conv_x,
    conv_bc,
    norm_gain,
):
    ctx = lax.axis_index("ctx")
    tp = lax.axis_index("tp")
    near = ctx % NEAR
    core = tp % 2
    group = tp // 2
    info = jnp.stack([(ctx // NEAR) * ROW, near, core, ctx * SHARD]).astype(jnp.int32)

    own = exchange_near(
        call(pair_kernel, [((NEAR, SHARD, 2 * HEAD), BF16)], (key_rows, value_rows)).reshape(
            ROW, 2 * HEAD
        )
    )
    bc_mine = lax.dynamic_slice(bc_input, (0, core, group, 0), (SHARD, 1, 1, STATE)).reshape(
        SHARD, STATE
    )
    taps_mine = lax.dynamic_slice(conv_bc, (0, core, group, 0), (4, 1, 1, STATE)).reshape(4, STATE)
    rim = from_shard_behind(bc_mine[SHARD - RIM :])
    packed = call(
        pack_kernel,
        [((NEAR, PACK_ROWS, HEAD), BF16)],
        (info, doc_lengths, queries, step_size, bc_mine, rim, taps_mine),
        smem=2,
        scratch=[pltpu.VMEM((RIM + SHARD, STATE), F32)],
    )
    back1 = from_row_behind(own, 1)
    back2 = from_row_behind(own, 2)
    back3 = from_row_behind(own[ROW - CHUNK :], 3)
    received = exchange_near(packed.reshape(NEAR * PACK_ROWS, HEAD)).reshape(
        NEAR, PACK_ROWS, HEAD
    )
    halo = from_row_behind(received[NEAR - 1, SHARD - RIM : SHARD], 1)
    other = with_partner(received[:, QUERY_ROWS:])
    mix, b_t, c_row, weigh, enter, enter_row, decays = call(
        mixing_kernel,
        [
            ((CHUNKS, 2, CHUNK, CHUNK), BF16),
            ((STATE, ROW), BF16),
            ((ROW, STATE), BF16),
            ((ROW, HEAD), F32),
            ((ROW, HEAD), F32),
            ((ROW, HEAD), F32),
            ((8, HEAD), F32),
        ],
        (info, doc_lengths, decay_rate, received, other),
        smem=3,
        flops=1 << 28,
    )
    x, states, handed = call(
        attend_kernel,
        [
            ((ROW, HEAD), BF16),
            ((CHUNKS, STATE, HEAD), BF16),
            ((STATE + 16, HEAD), BF16),
        ],
        (info, doc_lengths, received, halo, own, back1, back2, back3, conv_x, b_t, weigh, decays),
        smem=2,
        raw=(4, 5, 6, 7),
        scratch=[
            pltpu.VMEM((PAST + ROW, 2 * HEAD), BF16),
            pltpu.VMEM((ROW, HEAD), F32),
            pltpu.VMEM((ROW, HEAD), F32),
            pltpu.VMEM((ROW, HEAD), F32),
            pltpu.VMEM((ROW, HEAD), F32),
            pltpu.VMEM((RIM, HEAD), F32),
            pltpu.VMEM((RIM, HEAD), F32),
            pltpu.VMEM((RIM, HEAD), F32),
            pltpu.VMEM((RIM, HEAD), F32),
            pltpu.VMEM((RIM + ROW, HEAD), F32),
            pltpu.SemaphoreType.DMA((4,)),
        ],
        flops=1 << 30,
    )
    handed1 = from_row_behind(handed, 1)
    handed2 = from_row_behind(handed, 2)
    handed3 = from_row_behind(handed, 3)
    y_inner = call(
        inner_kernel,
        [((ROW, HEAD), F32)],
        (info, skip_gain, mix, x, c_row, states, enter),
        smem=2,
        flops=1 << 28,
    )
    y_row = call(
        carried_kernel,
        [((ROW, HEAD), BF16)],
        (y_inner, enter_row, c_row, handed1, handed2, handed3),
    )
    y_heads = exchange_near(y_row).reshape(NEAR, SHARD, HEAD)
    sums = call(square_kernel, [((SHARD, HEAD), F32)], (y_heads, gate_input))
    partner = with_partner(sums)
    return call(
        norm_kernel,
        [((SHARD, NEAR * HEAD), BF16)],
        (y_heads, gate_input, sums, partner, norm_gain.reshape(1, -1)),
    )


def solution(mesh):
    return jax.shard_map(
        on_device,
        mesh=mesh,
        in_specs=(
            P("ctx", "tp"),
            P("ctx", "tp"),
            P("ctx", "tp"),
            P(),
            P("ctx", "tp"),
            P("ctx", None, None, None),
            P("ctx", "tp"),
            P("tp"),
            P("tp"),
            P(None, "tp"),
            P(),
            P("tp"),
        ),
        out_specs=P("ctx", "tp"),
        check_vma=False,
    )
```

```python
import math

import jax
import jax.numpy as jnp
from jax import lax
from jax.experimental import pallas as pl
from jax.experimental.pallas import tpu as pltpu
from jax.sharding import PartitionSpec as P

EPSILON = 1e-05
NEGATIVE_FILL = -1e30
NEAR = 8
FAR = 4
SHARD = 128
ROW = NEAR * SHARD
CHUNK = 256
CHUNKS = ROW // CHUNK
HEAD = 128
STATE = 256
RIM = 16
PAST = 9 * CHUNK
STEPS_AT = SHARD + RIM
BC_AT = STEPS_AT + 16
PACK_ROWS = BC_AT + 2 * SHARD
EXP2_SCALE = math.log2(math.e) / math.sqrt(HEAD)
F32 = jnp.float32
BF16 = jnp.bfloat16


def near_groups():
    return [[x * NEAR + z for z in range(NEAR)] for x in range(FAR)]


def far_groups():
    return [[x * NEAR + z for x in range(FAR)] for z in range(NEAR)]


def exchange_near(x):
    return lax.all_to_all(x, "ctx", 0, 0, axis_index_groups=near_groups(), tiled=True)


def from_row_behind(x, by):
    pairs = [(x0 * NEAR + z, (x0 + by) * NEAR + z) for x0 in range(FAR - by) for z in range(NEAR)]
    return lax.ppermute(x, "ctx", pairs)


def from_shard_behind(x):
    return lax.ppermute(x, "ctx", [(i, i + 1) for i in range(NEAR * FAR - 1)])


def with_partner(x):
    count = lax.axis_size("tp")
    return lax.ppermute(x, "tp", [(t, t ^ 1) for t in range(count)])


def first_tokens(docs, pos):
    begin = jnp.int32(0)
    first = pos
    for d in range(docs.shape[0]):
        first = jnp.where(pos >= begin, begin, first)
        begin = begin + docs[d]
    return first


def columns_of(rows):
    count = rows[0].shape[1]
    rows = list(rows) + [jnp.zeros((1, count), F32)] * (8 - len(rows))
    return jnp.transpose(jnp.concatenate(rows, 0))


def silu(v):
    return v / (1.0 + jnp.exp(-v))


def pair_kernel(keys, values, out):
    for n in range(NEAR):
        out[n, :, 0:HEAD] = keys[...]
        out[n, :, HEAD:] = values[...]


def pack_kernel(info, docs, queries, steps, raw, rim, taps, out, ext):
    ext[0:RIM] = rim[:, NEAR * HEAD :].astype(F32)
    ext[RIM:] = raw[...].astype(F32)
    pos = info[3] + lax.broadcasted_iota(jnp.int32, (1, SHARD), 1)
    since = columns_of([(pos - first_tokens(docs, pos)).astype(F32)])[:, 0:1]
    acc = jnp.zeros((SHARD, STATE), F32)
    for m in range(4):
        part = ext[RIM - m : RIM - m + SHARD] * taps[3 - m : 4 - m]
        acc = acc + jnp.where(since >= m, part, 0.0)
    convolved = silu(acc).astype(BF16)
    wide = jnp.concatenate([steps[...], jnp.zeros((SHARD, HEAD - 2 * NEAR), F32)], 1)
    rows = jnp.transpose(wide)
    high = rows.astype(BF16).astype(F32)
    middle = (rows - high).astype(BF16).astype(F32)
    low = rows - high - middle
    for n in range(NEAR):
        out[n, 0:SHARD] = queries[:, n * HEAD : (n + 1) * HEAD]
        two = slice(2 * n, 2 * n + 2)
        out[n, SHARD:STEPS_AT] = rim[:, n * HEAD : (n + 1) * HEAD]
        out[n, STEPS_AT:BC_AT] = jnp.concatenate(
            [high[two], middle[two], low[two], jnp.zeros((10, HEAD), F32)], 0
        ).astype(BF16)
        out[n, BC_AT : BC_AT + SHARD] = convolved[:, 0:HEAD]
        out[n, BC_AT + SHARD :] = convolved[:, HEAD:]


def two_heads(first, second, shape):
    lane = lax.broadcasted_iota(jnp.int32, shape, 1)
    return jnp.where(lane < HEAD // 2, jnp.broadcast_to(first, shape), jnp.broadcast_to(second, shape))


def steps_of(received):
    pieces = []
    for s in range(NEAR):
        piece = received[s, STEPS_AT:BC_AT].astype(F32)
        pieces.append(piece[0:2] + piece[2:4] + piece[4:6])
    return jnp.concatenate(pieces, 1)


def decays_of(steps, rates, near):
    rate = jnp.concatenate(
        [jnp.full((1, ROW), rates[2 * near], F32), jnp.full((1, ROW), rates[2 * near + 1], F32)], 0
    )
    log_decay = jnp.concatenate([-rate * steps, jnp.zeros((6, ROW), F32)], 0)
    below = lax.broadcasted_iota(jnp.int32, (CHUNK, CHUNK), 0)
    across = lax.broadcasted_iota(jnp.int32, (CHUNK, CHUNK), 1)
    upper = jnp.where(below <= across, 1.0, 0.0).astype(F32)
    locals_ = [
        jnp.dot(
            log_decay[:, k * CHUNK : (k + 1) * CHUNK],
            upper,
            precision=lax.Precision.HIGHEST,
            preferred_element_type=F32,
        )[0:2]
        for k in range(CHUNKS)
    ]
    return locals_, [local[:, CHUNK - 1 : CHUNK] for local in locals_]


def prepare_kernel(info, docs, rates, received, other, b_t, weigh, decays):
    core_zero = info[2] == 0
    for s in range(NEAR):
        rows = slice(s * SHARD, (s + 1) * SHARD)
        for half in range(2):
            columns = slice(half * HEAD, (half + 1) * HEAD)
            at = slice(BC_AT + half * SHARD, BC_AT + (half + 1) * SHARD)
            from_other = slice(half * SHARD, (half + 1) * SHARD)
            b_values = jnp.where(core_zero, received[s, at], other[s, from_other])
            b_t[columns, rows] = jnp.transpose(b_values.astype(F32)).astype(BF16)
    steps = steps_of(received)
    locals_, totals = decays_of(steps, rates, info[1])
    row_start = info[0]
    pos = row_start + lax.broadcasted_iota(jnp.int32, (1, ROW), 1)
    first = first_tokens(docs, pos)
    decay_rows = []
    for k in range(CHUNKS):
        rows = slice(k * CHUNK, (k + 1) * CHUNK)
        last_start = first[:, (k + 1) * CHUNK - 1 : (k + 1) * CHUNK]
        gap = jnp.where(pos[:, rows] >= last_start, totals[k] - locals_[k], NEGATIVE_FILL)
        w = jnp.exp(gap) * steps[:, rows]
        columns = columns_of([w[0:1], w[1:2]])
        weigh[rows] = two_heads(columns[:, 0:1], columns[:, 1:2], (CHUNK, HEAD))
        crossing = jnp.where(last_start < row_start + k * CHUNK, jnp.exp(totals[k]), 0.0)
        decay_rows.append(two_heads(crossing[0:1], crossing[1:2], (1, HEAD)))
    whole = totals[0] + totals[1] + totals[2] + totals[3]
    last = jnp.where(first[:, ROW - 1 : ROW] < row_start, jnp.exp(whole), 0.0)
    decay_rows.append(two_heads(last[0:1], last[1:2], (1, HEAD)))
    decays[...] = jnp.concatenate(decay_rows + [jnp.zeros((3, HEAD), F32)], 0)


def attend_kernel(
    info,
    docs,
    received,
    own,
    back1,
    back2,
    back3,
    taps,
    b_t,
    weigh,
    decays,
    x_out,
    states,
    handed,
    keys,
    seen,
    top,
    total,
    summed,
    halo_seen,
    halo_top,
    halo_total,
    halo_summed,
    ext,
    sems,
):
    copies = [
        pltpu.make_async_copy(own, keys.at[pl.ds(PAST, ROW)], sems.at[0]),
        pltpu.make_async_copy(back1, keys.at[pl.ds(PAST - ROW, ROW)], sems.at[1]),
        pltpu.make_async_copy(back2, keys.at[pl.ds(PAST - 2 * ROW, ROW)], sems.at[2]),
        pltpu.make_async_copy(back3, keys.at[pl.ds(0, CHUNK)], sems.at[3]),
    ]
    for copy in copies:
        copy.start()
    row_start = info[0]
    near = info[1]
    pos = row_start + lax.broadcasted_iota(jnp.int32, (1, ROW), 1)
    first = first_tokens(docs, pos)
    columns = columns_of([(first - row_start).astype(F32), (pos - first).astype(F32)])
    since = columns[:, 1:2]
    seen[...] = jnp.broadcast_to(columns[:, 0:1], (ROW, HEAD))
    halo_pos = row_start - RIM + lax.broadcasted_iota(jnp.int32, (1, HEAD), 1)
    halo_first = columns_of([(first_tokens(docs, halo_pos) - row_start).astype(F32)])
    halo_seen[...] = jnp.broadcast_to(halo_first[0:RIM, 0:1], (RIM, HEAD))
    begin = jnp.int32(0)
    cross_start, cross_end = jnp.int32(0), jnp.int32(0)
    for d in range(docs.shape[0]):
        inside = begin <= row_start
        cross_start = jnp.where(inside, begin, cross_start)
        begin = begin + docs[d]
        cross_end = jnp.where(inside, begin, cross_end)
    lowest = lax.div(cross_start - row_start + PAST, jnp.int32(CHUNK))
    reached = cross_end - row_start

    def scores_of(query, block, seen_rows, causal):
        at = pl.ds(pl.multiple_of(block * CHUNK, CHUNK), CHUNK)
        raw = lax.dot_general(
            query, keys[at, 0:HEAD], (((1,), (1,)), ((), ())), preferred_element_type=F32
        )
        halves = []
        for half in range(2):
            offset = block * CHUNK - PAST + half * HEAD
            place = lax.broadcasted_iota(jnp.int32, (1, HEAD), 1) + offset
            visible = place.astype(F32) >= seen_rows
            if causal is not None:
                down = lax.broadcasted_iota(jnp.int32, (query.shape[0], HEAD), 0) + causal
                along = lax.broadcasted_iota(jnp.int32, (query.shape[0], HEAD), 1) + half * HEAD
                visible = visible & (along <= down)
            part = raw[:, half * HEAD : (half + 1) * HEAD]
            halves.append(jnp.where(visible, part, NEGATIVE_FILL))
        return halves, keys[at, HEAD:]

    def fold(query, block, seen_ref, top_ref, total_ref, summed_ref, rows, causal, fresh):
        (left, right), values = scores_of(query, block, seen_ref[rows], causal)
        largest = jnp.max(jnp.maximum(left, right), axis=1, keepdims=True)
        if fresh:
            new_top = jnp.broadcast_to(largest, left.shape)
        else:
            old_top = top_ref[rows]
            new_top = jnp.maximum(old_top, largest)
            factor = jnp.exp2((old_top - new_top) * EXP2_SCALE)
        left = jnp.exp2((left - new_top) * EXP2_SCALE)
        right = jnp.exp2((right - new_top) * EXP2_SCALE)
        weights = jnp.concatenate([left.astype(BF16), right.astype(BF16)], 1)
        product = jnp.dot(weights, values, preferred_element_type=F32)
        top_ref[rows] = new_top
        if fresh:
            total_ref[rows] = left + right
            summed_ref[rows] = product
        else:
            total_ref[rows] = total_ref[rows] * factor + (left + right)
            summed_ref[rows] = summed_ref[rows] * factor + product

    def query_of(i):
        return received[2 * i : 2 * i + 2, 0:SHARD, :].reshape(CHUNK, HEAD)

    def fold_row(i, block, causal, fresh):
        fold(
            query_of(i),
            block,
            seen,
            top,
            total,
            summed,
            slice(i * CHUNK, (i + 1) * CHUNK),
            causal,
            fresh,
        )

    def fold_halo(block, causal, fresh):
        fold(
            received[0, SHARD:STEPS_AT],
            block,
            halo_seen,
            halo_top,
            halo_total,
            halo_summed,
            slice(0, RIM),
            causal,
            fresh,
        )

    own_block = PAST // CHUNK
    copies[0].wait()
    for back in range(CHUNKS):
        for i in range(back, CHUNKS):
            fold_row(i, own_block + i - back, 0 if back == 0 else None, back == 0)
    for copy in copies[1:]:
        copy.wait()
    fold_halo(own_block - 1, CHUNK - RIM, True)

    def earlier(count):
        def visit(n, carry):
            block = own_block - 1 - n
            for i in range(count):
                fold_row(i, block, None, False)

            @pl.when(n > 0)
            def _():
                fold_halo(block, None, False)

            return carry

        lax.fori_loop(0, own_block - lowest, visit, 0)

    @pl.when(reached <= CHUNK)
    def _():
        earlier(1)

    @pl.when((reached > CHUNK) & (reached <= 2 * CHUNK))
    def _():
        earlier(2)

    @pl.when(reached > 2 * CHUNK)
    def _():
        earlier(CHUNKS)

    def finish(total_ref, summed_ref):
        whole = jnp.sum(total_ref[...], axis=1, keepdims=True)
        return (summed_ref[...] / whole).astype(BF16).astype(F32)

    ext[0:RIM] = finish(halo_total, halo_summed)
    ext[RIM:] = finish(total, summed)
    own_taps = taps[:, pl.ds(pl.multiple_of(near * HEAD, HEAD), HEAD)]
    state = jnp.zeros((STATE, HEAD), F32)
    for k in range(CHUNKS):
        rows = slice(k * CHUNK, (k + 1) * CHUNK)
        acc = jnp.zeros((CHUNK, HEAD), F32)
        for m in range(4):
            part = ext[RIM - m + k * CHUNK : RIM - m + (k + 1) * CHUNK] * own_taps[3 - m : 4 - m]
            acc = acc + jnp.where(since[rows] >= m, part, 0.0)
        x = silu(acc).astype(BF16)
        x_out[rows] = x
        states[k] = state.astype(BF16)
        weighed = (x.astype(F32) * weigh[rows]).astype(BF16)
        state = state * decays[k : k + 1] + jnp.dot(
            b_t[:, rows], weighed, preferred_element_type=F32
        )
    decay = decays[CHUNKS : CHUNKS + 1]
    high = decay.astype(BF16).astype(F32)
    tail = jnp.concatenate([high, decay - high, jnp.zeros((14, HEAD), F32)], 0).astype(BF16)
    state = state.astype(BF16)
    for r in range(FAR):
        handed[r, 0:STATE] = state
        handed[r, STATE:] = tail


def inner_kernel(
    info, docs, rates, skip, received, other, b_t, x_in, states, y_out, enter_row, c_out
):
    near = info[1]
    core_zero = info[2] == 0
    for s in range(NEAR):
        rows = slice(s * SHARD, (s + 1) * SHARD)
        for half in range(2):
            at = slice(BC_AT + half * SHARD, BC_AT + (half + 1) * SHARD)
            from_other = slice(half * SHARD, (half + 1) * SHARD)
            c_out[rows, half * HEAD : (half + 1) * HEAD] = jnp.where(
                core_zero, other[s, from_other], received[s, at]
            )
    steps = steps_of(received)
    locals_, totals = decays_of(steps, rates, near)
    row_start = info[0]
    pos = row_start + lax.broadcasted_iota(jnp.int32, (1, ROW), 1)
    first = first_tokens(docs, pos)
    below = lax.broadcasted_iota(jnp.int32, (CHUNK, CHUNK), 0)
    across = lax.broadcasted_iota(jnp.int32, (CHUNK, CHUNK), 1)
    causal = across <= below
    place = across.astype(F32)
    gain = two_heads(skip[2 * near], skip[2 * near + 1], (1, HEAD))
    shape = (CHUNK, HEAD)
    before = jnp.zeros((2, 1), F32)
    for k in range(CHUNKS):
        rows = slice(k * CHUNK, (k + 1) * CHUNK)
        chunk_start = row_start + k * CHUNK
        local = locals_[k]
        e_chunk = jnp.exp(jnp.where(first[:, rows] < chunk_start, local, NEGATIVE_FILL))
        e_row = jnp.exp(jnp.where(first[:, rows] < row_start, before + local, NEGATIVE_FILL))
        before = before + totals[k]
        columns = jnp.transpose(jnp.concatenate([e_chunk, e_row, local, jnp.zeros((2, CHUNK), F32)], 0))
        since = columns_of([(first[:, rows] - chunk_start).astype(F32)])[:, 0:1]
        enter_row[rows] = two_heads(columns[:, 2:3], columns[:, 3:4], shape)
        gram = jnp.dot(c_out[rows], b_t[:, rows], preferred_element_type=F32)
        visible = causal & (place >= since)
        x = x_in[rows]
        halves = []
        for h in range(2):
            gap = jnp.where(visible, columns[:, 4 + h : 5 + h] - local[h : h + 1], NEGATIVE_FILL)
            mix = (gram * jnp.exp(gap) * steps[h : h + 1, rows]).astype(BF16)
            halves.append(jnp.dot(mix, x, preferred_element_type=F32))
        lane = lax.broadcasted_iota(jnp.int32, shape, 1)
        y = jnp.where(lane < HEAD // 2, halves[0], halves[1]) + x.astype(F32) * gain
        if k > 0:
            carried = jnp.dot(c_out[rows], states[k], preferred_element_type=F32)
            y = y + two_heads(columns[:, 0:1], columns[:, 1:2], shape) * carried
        y_out[rows] = y


def carried_kernel(info, y_in, enter_row, c_in, handed, y_out):
    entering = jnp.zeros((STATE, HEAD), F32)
    for r in range(FAR - 1):
        tail = handed[r, STATE:].astype(F32)
        following = entering * (tail[0:1] + tail[1:2]) + handed[r, 0:STATE].astype(F32)
        entering = jnp.where(r * ROW < info[0], following, entering)
    entering = entering.astype(BF16)
    for k in range(CHUNKS):
        rows = slice(k * CHUNK, (k + 1) * CHUNK)
        carried = jnp.dot(c_in[rows], entering, preferred_element_type=F32)
        y_out[rows] = (y_in[rows] + enter_row[rows] * carried).astype(BF16)


def gated_of(y, gate, h):
    return y[h].astype(F32) * silu(gate[:, h * HEAD : (h + 1) * HEAD].astype(F32))


def square_kernel(y, gate, sums):
    acc = jnp.zeros((SHARD, HEAD), F32)
    for h in range(NEAR):
        gated = gated_of(y, gate, h)
        acc = acc + gated * gated
    sums[...] = jnp.broadcast_to(jnp.sum(acc, axis=1, keepdims=True), (SHARD, HEAD))


def norm_kernel(y, gate, sums, partner, gain, out):
    mean = (sums[...] + partner[...]) / (2.0 * NEAR * HEAD)
    scale = lax.rsqrt(mean + EPSILON)
    for h in range(NEAR):
        columns = slice(h * HEAD, (h + 1) * HEAD)
        out[:, columns] = (gated_of(y, gate, h) * scale * gain[:, columns]).astype(BF16)


def call(kernel, outs, args, smem=0, raw=(), scratch=(), flops=0, mib=16):
    specs = []
    for n in range(len(args)):
        if n < smem:
            specs.append(pl.BlockSpec(memory_space=pltpu.SMEM))
        elif n in raw:
            specs.append(pl.BlockSpec(memory_space=pl.ANY))
        else:
            specs.append(pl.BlockSpec(memory_space=pltpu.VMEM))
    single = len(outs) == 1
    shapes = [jax.ShapeDtypeStruct(shape, kind) for shape, kind in outs]
    out_specs = [pl.BlockSpec(memory_space=pltpu.VMEM)] * len(outs)
    return pl.pallas_call(
        kernel,
        out_shape=shapes[0] if single else shapes,
        in_specs=specs,
        out_specs=out_specs[0] if single else out_specs,
        scratch_shapes=list(scratch),
        compiler_params=pltpu.CompilerParams(vmem_limit_bytes=mib * 1024 * 1024),
        cost_estimate=pl.CostEstimate(flops=flops, bytes_accessed=1 << 21, transcendentals=0),
    )(*args)


def on_device(
    queries,
    key_rows,
    value_rows,
    doc_lengths,
    gate_input,
    bc_input,
    step_size,
    decay_rate,
    skip_gain,
    conv_x,
    conv_bc,
    norm_gain,
):
    ctx = lax.axis_index("ctx")
    tp = lax.axis_index("tp")
    near = ctx % NEAR
    core = tp % 2
    group = tp // 2
    info = jnp.stack([(ctx // NEAR) * ROW, near, core, ctx * SHARD]).astype(jnp.int32)

    bc_mine = lax.dynamic_slice(bc_input, (0, core, group, 0), (SHARD, 1, 1, STATE)).reshape(
        SHARD, STATE
    )
    taps_mine = lax.dynamic_slice(conv_bc, (0, core, group, 0), (4, 1, 1, STATE)).reshape(4, STATE)
    rim = from_shard_behind(jnp.concatenate([queries[SHARD - RIM :], bc_mine[SHARD - RIM :]], 1))
    own = exchange_near(
        call(pair_kernel, [((NEAR, SHARD, 2 * HEAD), BF16)], (key_rows, value_rows)).reshape(
            ROW, 2 * HEAD
        )
    )
    own, queries = lax.optimization_barrier((own, queries))
    packed = call(
        pack_kernel,
        [((NEAR, PACK_ROWS, HEAD), BF16)],
        (info, doc_lengths, queries, step_size, bc_mine, rim, taps_mine),
        smem=2,
        scratch=[pltpu.VMEM((RIM + SHARD, STATE), F32)],
    )
    back1 = from_row_behind(own, 1)
    back2 = from_row_behind(own, 2)
    back3 = from_row_behind(own[ROW - CHUNK :], 3)
    received = exchange_near(packed.reshape(NEAR * PACK_ROWS, HEAD)).reshape(
        NEAR, PACK_ROWS, HEAD
    )
    received, back1, back2, back3 = lax.optimization_barrier((received, back1, back2, back3))
    other = with_partner(received[:, BC_AT:])
    b_t, weigh, decays = call(
        prepare_kernel,
        [((STATE, ROW), BF16), ((ROW, HEAD), F32), ((8, HEAD), F32)],
        (info, doc_lengths, decay_rate, received, other),
        smem=3,
    )
    x, states, handed = call(
        attend_kernel,
        [
            ((ROW, HEAD), BF16),
            ((CHUNKS, STATE, HEAD), BF16),
            ((FAR, STATE + 16, HEAD), BF16),
        ],
        (info, doc_lengths, received, own, back1, back2, back3, conv_x, b_t, weigh, decays),
        smem=2,
        raw=(3, 4, 5, 6),
        scratch=[
            pltpu.VMEM((PAST + ROW, 2 * HEAD), BF16),
            pltpu.VMEM((ROW, HEAD), F32),
            pltpu.VMEM((ROW, HEAD), F32),
            pltpu.VMEM((ROW, HEAD), F32),
            pltpu.VMEM((ROW, HEAD), F32),
            pltpu.VMEM((RIM, HEAD), F32),
            pltpu.VMEM((RIM, HEAD), F32),
            pltpu.VMEM((RIM, HEAD), F32),
            pltpu.VMEM((RIM, HEAD), F32),
            pltpu.VMEM((RIM + ROW, HEAD), F32),
            pltpu.SemaphoreType.DMA((4,)),
        ],
        flops=1 << 30,
        mib=24,
    )
    handed = lax.all_to_all(
        handed.reshape(FAR * (STATE + 16), HEAD),
        "ctx",
        0,
        0,
        axis_index_groups=far_groups(),
        tiled=True,
    ).reshape(FAR, STATE + 16, HEAD)
    y_inner, enter_row, c_row = call(
        inner_kernel,
        [((ROW, HEAD), F32), ((ROW, HEAD), F32), ((ROW, STATE), BF16)],
        (info, doc_lengths, decay_rate, skip_gain, received, other, b_t, x, states),
        smem=4,
        flops=1 << 30,
    )
    y_row = call(
        carried_kernel,
        [((ROW, HEAD), BF16)],
        (info, y_inner, enter_row, c_row, handed),
        smem=1,
    )
    y_heads = exchange_near(y_row).reshape(NEAR, SHARD, HEAD)
    sums = call(square_kernel, [((SHARD, HEAD), F32)], (y_heads, gate_input))
    partner = with_partner(sums)
    return call(
        norm_kernel,
        [((SHARD, NEAR * HEAD), BF16)],
        (y_heads, gate_input, sums, partner, norm_gain.reshape(1, -1)),
    )


def solution(mesh):
    return jax.shard_map(
        on_device,
        mesh=mesh,
        in_specs=(
            P("ctx", "tp"),
            P("ctx", "tp"),
            P("ctx", "tp"),
            P(),
            P("ctx", "tp"),
            P("ctx", None, None, None),
            P("ctx", "tp"),
            P("tp"),
            P("tp"),
            P(None, "tp"),
            P(),
            P("tp"),
        ),
        out_specs=P("ctx", "tp"),
        check_vma=False,
    )
```

```python
import math

import jax
import jax.numpy as jnp
from jax import lax
from jax.experimental import pallas as pl
from jax.experimental.pallas import tpu as pltpu
from jax.sharding import PartitionSpec as P

EPSILON = 1e-05
NEGATIVE_FILL = -1e30
NEAR = 8
FAR = 4
SHARD = 128
ROW = NEAR * SHARD
CHUNK = 256
CHUNKS = ROW // CHUNK
HEAD = 128
STATE = 256
RIM = 16
PAST = 10 * CHUNK
WIDE = 256
STEPS_AT = SHARD + RIM
BC_AT = STEPS_AT + 16
PACK_ROWS = BC_AT + 2 * SHARD
EXP2_SCALE = math.log2(math.e) / math.sqrt(HEAD)
F32 = jnp.float32
BF16 = jnp.bfloat16


def near_groups():
    return [[x * NEAR + z for z in range(NEAR)] for x in range(FAR)]


def far_groups():
    return [[x * NEAR + z for x in range(FAR)] for z in range(NEAR)]


def exchange_near(x):
    return lax.all_to_all(x, "ctx", 0, 0, axis_index_groups=near_groups(), tiled=True)


def from_row_behind(x, by):
    pairs = [(x0 * NEAR + z, (x0 + by) * NEAR + z) for x0 in range(FAR - by) for z in range(NEAR)]
    return lax.ppermute(x, "ctx", pairs)


def from_shard_behind(x):
    return lax.ppermute(x, "ctx", [(i, i + 1) for i in range(NEAR * FAR - 1)])


def with_partner(x):
    count = lax.axis_size("tp")
    return lax.ppermute(x, "tp", [(t, t ^ 1) for t in range(count)])


def first_tokens(docs, pos):
    begin = jnp.int32(0)
    first = pos
    for d in range(docs.shape[0]):
        first = jnp.where(pos >= begin, begin, first)
        begin = begin + docs[d]
    return first


def columns_of(rows):
    count = rows[0].shape[1]
    rows = list(rows) + [jnp.zeros((1, count), F32)] * (8 - len(rows))
    return jnp.transpose(jnp.concatenate(rows, 0))


def silu(v):
    return v / (1.0 + jnp.exp(-v))


def pair_kernel(keys, values, out, sems):
    copies = []
    for n in range(NEAR):
        copies.append(pltpu.make_async_copy(keys, out.at[n, :, pl.ds(0, HEAD)], sems.at[2 * n]))
        copies.append(
            pltpu.make_async_copy(values, out.at[n, :, pl.ds(HEAD, HEAD)], sems.at[2 * n + 1])
        )
    for copy in copies:
        copy.start()
    for copy in copies:
        copy.wait()


def pack_kernel(info, docs, queries, steps, raw, rim, taps, out, ext):
    ext[0:RIM] = rim[:, NEAR * HEAD :].astype(F32)
    ext[RIM:] = raw[...].astype(F32)
    pos = info[3] + lax.broadcasted_iota(jnp.int32, (1, SHARD), 1)
    since = columns_of([(pos - first_tokens(docs, pos)).astype(F32)])[:, 0:1]
    acc = jnp.zeros((SHARD, STATE), F32)
    for m in range(4):
        part = ext[RIM - m : RIM - m + SHARD] * taps[3 - m : 4 - m]
        acc = acc + jnp.where(since >= m, part, 0.0)
    convolved = silu(acc).astype(BF16)
    wide = jnp.concatenate([steps[...], jnp.zeros((SHARD, HEAD - 2 * NEAR), F32)], 1)
    rows = jnp.transpose(wide)
    high = rows.astype(BF16).astype(F32)
    middle = (rows - high).astype(BF16).astype(F32)
    low = rows - high - middle
    for n in range(NEAR):
        out[n, 0:SHARD] = queries[:, n * HEAD : (n + 1) * HEAD]
        two = slice(2 * n, 2 * n + 2)
        out[n, SHARD:STEPS_AT] = rim[:, n * HEAD : (n + 1) * HEAD]
        out[n, STEPS_AT:BC_AT] = jnp.concatenate(
            [high[two], middle[two], low[two], jnp.zeros((10, HEAD), F32)], 0
        ).astype(BF16)
        out[n, BC_AT : BC_AT + SHARD] = convolved[:, 0:HEAD]
        out[n, BC_AT + SHARD :] = convolved[:, HEAD:]


def two_heads(first, second, shape):
    lane = lax.broadcasted_iota(jnp.int32, shape, 1)
    return jnp.where(lane < HEAD // 2, jnp.broadcast_to(first, shape), jnp.broadcast_to(second, shape))


def steps_of(received):
    pieces = []
    for s in range(NEAR):
        piece = received[s, STEPS_AT:BC_AT].astype(F32)
        pieces.append(piece[0:2] + piece[2:4] + piece[4:6])
    return jnp.concatenate(pieces, 1)


def decays_of(steps, rates, near):
    rate = jnp.concatenate(
        [jnp.full((1, ROW), rates[2 * near], F32), jnp.full((1, ROW), rates[2 * near + 1], F32)], 0
    )
    log_decay = jnp.concatenate([-rate * steps, jnp.zeros((6, ROW), F32)], 0)
    below = lax.broadcasted_iota(jnp.int32, (CHUNK, CHUNK), 0)
    across = lax.broadcasted_iota(jnp.int32, (CHUNK, CHUNK), 1)
    upper = jnp.where(below <= across, 1.0, 0.0).astype(F32)
    locals_ = [
        jnp.dot(
            log_decay[:, k * CHUNK : (k + 1) * CHUNK],
            upper,
            precision=lax.Precision.HIGHEST,
            preferred_element_type=F32,
        )[0:2]
        for k in range(CHUNKS)
    ]
    return locals_, [local[:, CHUNK - 1 : CHUNK] for local in locals_]


def weights_kernel(info, docs, rates, received, weigh, decays, since, seen):
    steps = steps_of(received)
    locals_, totals = decays_of(steps, rates, info[1])
    row_start = info[0]
    pos = row_start + lax.broadcasted_iota(jnp.int32, (1, ROW), 1)
    first = first_tokens(docs, pos)
    decay_rows = []
    for k in range(CHUNKS):
        rows = slice(k * CHUNK, (k + 1) * CHUNK)
        last_start = first[:, (k + 1) * CHUNK - 1 : (k + 1) * CHUNK]
        gap = jnp.where(pos[:, rows] >= last_start, totals[k] - locals_[k], NEGATIVE_FILL)
        w = jnp.exp(gap) * steps[:, rows]
        begin = first[:, rows]
        columns = columns_of(
            [w[0:1], w[1:2], (pos[:, rows] - begin).astype(F32), (begin - row_start).astype(F32)]
        )
        weigh[rows] = two_heads(columns[:, 0:1], columns[:, 1:2], (CHUNK, HEAD))
        since[rows] = jnp.broadcast_to(columns[:, 2:3], (CHUNK, HEAD))
        seen[rows] = jnp.broadcast_to(columns[:, 3:4], (CHUNK, HEAD))
        crossing = jnp.where(last_start < row_start + k * CHUNK, jnp.exp(totals[k]), 0.0)
        decay_rows.append(jnp.broadcast_to(crossing, (2, STATE)))
    whole = totals[0] + totals[1] + totals[2] + totals[3]
    last = jnp.where(first[:, ROW - 1 : ROW] < row_start, jnp.exp(whole), 0.0)
    decay_rows.append(jnp.broadcast_to(last, (2, STATE)))
    decays[...] = jnp.concatenate(decay_rows + [jnp.zeros((6, STATE), F32)], 0)


def two_head_rows(pair):
    shape = (HEAD, STATE)
    channel = lax.broadcasted_iota(jnp.int32, shape, 0)
    return jnp.where(
        channel < HEAD // 2,
        jnp.broadcast_to(pair[0:1], shape),
        jnp.broadcast_to(pair[1:2], shape),
    )


def dot_rows(left, right):
    return lax.dot_general(left, right, (((1,), (1,)), ((), ())), preferred_element_type=F32)


def chunk_of(choose_mine, received, other, k):
    halves = []
    two = slice(2 * k, 2 * k + 2)
    for half in range(2):
        mine = received[two, BC_AT + half * SHARD : BC_AT + (half + 1) * SHARD]
        theirs = other[two, half * SHARD : (half + 1) * SHARD]
        halves.append(jnp.where(choose_mine, mine, theirs))
    return jnp.concatenate([half.reshape(CHUNK, HEAD) for half in halves], 1)


def attend_kernel(
    info,
    docs,
    received,
    own,
    back1,
    back2a,
    back2b,
    back3,
    seen,
    attended,
    top,
    total,
    summed,
    halo_seen,
    halo_top,
    halo_total,
    halo_summed,
):
    row_start = info[0]
    halo_pos = row_start - RIM + lax.broadcasted_iota(jnp.int32, (1, HEAD), 1)
    halo_first = columns_of([(first_tokens(docs, halo_pos) - row_start).astype(F32)])
    halo_seen[...] = jnp.broadcast_to(halo_first[0:RIM, 0:1], (RIM, HEAD))
    begin = jnp.int32(0)
    cross_start, cross_end = jnp.int32(0), jnp.int32(0)
    for d in range(docs.shape[0]):
        inside = begin <= row_start
        cross_start = jnp.where(inside, begin, cross_start)
        begin = begin + docs[d]
        cross_end = jnp.where(inside, begin, cross_end)
    reached = cross_end - row_start
    wide_blocks = PAST // WIDE
    lowest = lax.div(cross_start - row_start + PAST, jnp.int32(WIDE))

    def masked(raw, offset, seen_rows, diagonal):
        count = raw.shape[0]
        slabs = []
        for n in range(raw.shape[1] // HEAD):
            place = lax.broadcasted_iota(jnp.int32, (1, HEAD), 1) + (offset + n * HEAD)
            visible = place.astype(F32) >= seen_rows
            if diagonal is not None:
                down = lax.broadcasted_iota(jnp.int32, (count, HEAD), 0) + diagonal
                along = lax.broadcasted_iota(jnp.int32, (count, HEAD), 1) + n * HEAD
                visible = visible & (along <= down)
            slabs.append(jnp.where(visible, raw[:, n * HEAD : (n + 1) * HEAD], NEGATIVE_FILL))
        return slabs

    def largest_of(slabs):
        most = slabs[0]
        for slab in slabs[1:]:
            most = jnp.maximum(most, slab)
        return jnp.max(most, axis=1, keepdims=True)

    def weighed(slabs, new_top):
        parts, sums = [], None
        for slab in slabs:
            weight = jnp.exp2((slab - new_top) * EXP2_SCALE)
            sums = weight if sums is None else sums + weight
            parts.append(weight.astype(BF16))
        return sums, parts

    def fold(query, keys, block, within, seen_ref, top_ref, total_ref, summed_ref, rows, diagonal):
        at = pl.ds(pl.multiple_of(within * WIDE, WIDE), WIDE)
        raw = dot_rows(query, keys[at, 0:HEAD])
        slabs = masked(raw, block * WIDE - PAST, seen_ref[rows], diagonal)
        old_top = top_ref[rows]
        new_top = jnp.maximum(old_top, largest_of(slabs))
        factor = jnp.exp2((old_top - new_top) * EXP2_SCALE)
        sums, parts = weighed(slabs, new_top)
        product = jnp.dot(
            jnp.concatenate(parts, 1), keys[at, HEAD:], preferred_element_type=F32
        )
        top_ref[rows] = new_top
        total_ref[rows] = total_ref[rows] * factor + sums
        summed_ref[rows] = summed_ref[rows] * factor + product

    raws, weights = [], [[] for _ in range(CHUNKS)]
    for j in range(CHUNKS):
        query = received[2 * j :, 0:SHARD, :].reshape(ROW - j * CHUNK, HEAD)
        at = slice(j * CHUNK, (j + 1) * CHUNK)
        raws.append(dot_rows(query, own[at, 0:HEAD]))
    for i in range(CHUNKS):
        rows = slice(i * CHUNK, (i + 1) * CHUNK)
        slabs = []
        for j in range(i + 1):
            raw = raws[j][(i - j) * CHUNK : (i - j + 1) * CHUNK]
            slabs += masked(raw, j * CHUNK, seen[rows], 0 if i == j else None)
        first_top = jnp.broadcast_to(largest_of(slabs), (CHUNK, HEAD))
        sums, parts = weighed(slabs, first_top)
        top[rows] = first_top
        total[rows] = sums
        for j in range(i + 1):
            weights[j].append(jnp.concatenate(parts[2 * j : 2 * j + 2], 1))
    for j in range(CHUNKS):
        values = own[j * CHUNK : (j + 1) * CHUNK, HEAD:]
        product = jnp.dot(jnp.concatenate(weights[j], 0), values, preferred_element_type=F32)
        rows = slice(j * CHUNK, ROW)
        summed[rows] = product if j == 0 else summed[rows] + product
    halo_top[...] = jnp.full((RIM, HEAD), NEGATIVE_FILL, F32)
    halo_total[...] = jnp.zeros((RIM, HEAD), F32)
    halo_summed[...] = jnp.zeros((RIM, HEAD), F32)

    def earlier(count):
        query = received[0 : 2 * count, 0:SHARD, :].reshape(count * CHUNK, HEAD)
        for keys, begin in ((back1, 6), (back2b, 4), (back2a, 2), (back3, 0)):
            blocks = keys.shape[0] // WIDE

            def visit(n, carry):
                within = blocks - 1 - n
                block = begin + within
                fold(
                    query, keys, block, within, seen, top, total, summed, slice(0, count * CHUNK), None
                )
                fold(
                    received[0, SHARD:STEPS_AT],
                    keys,
                    block,
                    within,
                    halo_seen,
                    halo_top,
                    halo_total,
                    halo_summed,
                    slice(0, RIM),
                    (PAST - RIM) - block * WIDE,
                )
                return carry

            lax.fori_loop(0, jnp.clip(begin + blocks - lowest, 0, blocks), visit, 0)

    @pl.when(reached <= CHUNK)
    def _():
        earlier(1)

    @pl.when((reached > CHUNK) & (reached <= 2 * CHUNK))
    def _():
        earlier(2)

    @pl.when(reached > 2 * CHUNK)
    def _():
        earlier(CHUNKS)

    def finish(total_ref, summed_ref):
        whole = jnp.sum(total_ref[...], axis=1, keepdims=True)
        return (summed_ref[...] / jnp.maximum(whole, 0.5)).astype(BF16)

    attended[0:RIM] = finish(halo_total, halo_summed)
    attended[RIM:] = finish(total, summed)


def scan_kernel(
    info, attended, received, other, taps, weigh, decays, since, x_out, states, handed, ext
):
    ext[...] = attended[...].astype(F32)
    near = info[1]
    own_taps = taps[:, pl.ds(pl.multiple_of(near * HEAD, HEAD), HEAD)]
    core_zero = info[2] == 0
    state = jnp.zeros((HEAD, STATE), F32)
    for k in range(CHUNKS):
        rows = slice(k * CHUNK, (k + 1) * CHUNK)
        acc = jnp.zeros((CHUNK, HEAD), F32)
        for m in range(4):
            part = ext[RIM - m + k * CHUNK : RIM - m + (k + 1) * CHUNK] * own_taps[3 - m : 4 - m]
            acc = acc + jnp.where(since[rows] >= m, part, 0.0)
        x = silu(acc).astype(BF16)
        x_out[rows] = x
        states[k] = state.astype(BF16)
        weighed = (x.astype(F32) * weigh[rows]).astype(BF16)
        added = lax.dot_general(
            weighed,
            chunk_of(core_zero, received, other, k),
            (((0,), (0,)), ((), ())),
            preferred_element_type=F32,
        )
        state = state * two_head_rows(decays[2 * k : 2 * k + 2]) + added
    decay = decays[2 * CHUNKS : 2 * CHUNKS + 2]
    high = decay.astype(BF16).astype(F32)
    tail = jnp.concatenate([high, decay - high, jnp.zeros((12, STATE), F32)], 0).astype(BF16)
    state = state.astype(BF16)
    for r in range(FAR):
        handed[r, 0:HEAD] = state
        handed[r, HEAD:] = tail


def inner_kernel(
    info, docs, rates, skip, received, other, x_in, states, y_out, enter_row, c_out
):
    near = info[1]
    core_zero = info[2] == 0
    steps = steps_of(received)
    locals_, totals = decays_of(steps, rates, near)
    row_start = info[0]
    pos = row_start + lax.broadcasted_iota(jnp.int32, (1, ROW), 1)
    first = first_tokens(docs, pos)
    below = lax.broadcasted_iota(jnp.int32, (CHUNK, CHUNK), 0)
    across = lax.broadcasted_iota(jnp.int32, (CHUNK, CHUNK), 1)
    causal = across <= below
    place = across.astype(F32)
    gain = two_heads(skip[2 * near], skip[2 * near + 1], (1, HEAD))
    shape = (CHUNK, HEAD)
    before = jnp.zeros((2, 1), F32)
    for k in range(CHUNKS):
        rows = slice(k * CHUNK, (k + 1) * CHUNK)
        chunk_start = row_start + k * CHUNK
        local = locals_[k]
        e_chunk = jnp.exp(jnp.where(first[:, rows] < chunk_start, local, NEGATIVE_FILL))
        e_row = jnp.exp(jnp.where(first[:, rows] < row_start, before + local, NEGATIVE_FILL))
        before = before + totals[k]
        columns = jnp.transpose(jnp.concatenate([e_chunk, e_row, local, jnp.zeros((2, CHUNK), F32)], 0))
        since = columns_of([(first[:, rows] - chunk_start).astype(F32)])[:, 0:1]
        enter_row[rows] = two_heads(columns[:, 2:3], columns[:, 3:4], shape)
        c_values = chunk_of(jnp.logical_not(core_zero), received, other, k)
        c_out[rows] = c_values
        gram = dot_rows(c_values, chunk_of(core_zero, received, other, k))
        visible = causal & (place >= since)
        x = x_in[rows]
        halves = []
        for h in range(2):
            gap = jnp.where(visible, columns[:, 4 + h : 5 + h] - local[h : h + 1], NEGATIVE_FILL)
            mix = (gram * jnp.exp(gap) * steps[h : h + 1, rows]).astype(BF16)
            halves.append(jnp.dot(mix, x, preferred_element_type=F32))
        lane = lax.broadcasted_iota(jnp.int32, shape, 1)
        y = jnp.where(lane < HEAD // 2, halves[0], halves[1]) + x.astype(F32) * gain
        if k > 0:
            carried = dot_rows(c_values, states[k])
            y = y + two_heads(columns[:, 0:1], columns[:, 1:2], shape) * carried
        y_out[rows] = y


def carried_kernel(info, y_in, enter_row, c_in, handed, y_out):
    entering = jnp.zeros((HEAD, STATE), F32)
    for r in range(FAR - 1):
        tail = handed[r, HEAD:].astype(F32)
        decay = two_head_rows(tail[0:2] + tail[2:4])
        following = entering * decay + handed[r, 0:HEAD].astype(F32)
        entering = jnp.where(r * ROW < info[0], following, entering)
    entering = entering.astype(BF16)
    for k in range(CHUNKS):
        rows = slice(k * CHUNK, (k + 1) * CHUNK)
        carried = dot_rows(c_in[rows], entering)
        y_out[rows] = (y_in[rows] + enter_row[rows] * carried).astype(BF16)


def gated_of(y, gate, h):
    return y[h].astype(F32) * silu(gate[:, h * HEAD : (h + 1) * HEAD].astype(F32))


def square_kernel(y, gate, sums):
    acc = jnp.zeros((SHARD, HEAD), F32)
    for h in range(NEAR):
        gated = gated_of(y, gate, h)
        acc = acc + gated * gated
    sums[...] = jnp.broadcast_to(jnp.sum(acc, axis=1, keepdims=True), (SHARD, HEAD))


def norm_kernel(y, gate, sums, partner, gain, out):
    mean = (sums[...] + partner[...]) / (2.0 * NEAR * HEAD)
    scale = lax.rsqrt(mean + EPSILON)
    for h in range(NEAR):
        columns = slice(h * HEAD, (h + 1) * HEAD)
        out[:, columns] = (gated_of(y, gate, h) * scale * gain[:, columns]).astype(BF16)


def call(kernel, outs, args, smem=0, raw=(), raw_out=False, scratch=(), flops=0, mib=16):
    specs = []
    for n in range(len(args)):
        if n < smem:
            specs.append(pl.BlockSpec(memory_space=pltpu.SMEM))
        elif n in raw:
            specs.append(pl.BlockSpec(memory_space=pl.ANY))
        else:
            specs.append(pl.BlockSpec(memory_space=pltpu.VMEM))
    single = len(outs) == 1
    shapes = [jax.ShapeDtypeStruct(shape, kind) for shape, kind in outs]
    out_specs = [pl.BlockSpec(memory_space=pl.ANY if raw_out else pltpu.VMEM)] * len(outs)
    return pl.pallas_call(
        kernel,
        out_shape=shapes[0] if single else shapes,
        in_specs=specs,
        out_specs=out_specs[0] if single else out_specs,
        scratch_shapes=list(scratch),
        compiler_params=pltpu.CompilerParams(vmem_limit_bytes=mib * 1024 * 1024),
        cost_estimate=pl.CostEstimate(flops=flops, bytes_accessed=1 << 21, transcendentals=0),
    )(*args)


def run_attend(info, docs, received, own, back1, back2a, back2b, back3, seen):
    return call(
        attend_kernel,
        [((RIM + ROW, HEAD), BF16)],
        (info, docs, received, own, back1, back2a, back2b, back3, seen),
        smem=2,
        scratch=[
            pltpu.VMEM((ROW, HEAD), F32),
            pltpu.VMEM((ROW, HEAD), F32),
            pltpu.VMEM((ROW, HEAD), F32),
            pltpu.VMEM((RIM, HEAD), F32),
            pltpu.VMEM((RIM, HEAD), F32),
            pltpu.VMEM((RIM, HEAD), F32),
            pltpu.VMEM((RIM, HEAD), F32),
        ],
        flops=1 << 32,
        mib=24,
    )


def run_scan(info, attended, received, other, taps, weigh, decays, since):
    return call(
        scan_kernel,
        [
            ((ROW, HEAD), BF16),
            ((CHUNKS, HEAD, STATE), BF16),
            ((FAR, HEAD + 16, STATE), BF16),
        ],
        (info, attended, received, other, taps, weigh, decays, since),
        smem=1,
        scratch=[pltpu.VMEM((RIM + ROW, HEAD), F32)],
    )


def on_device(
    queries,
    key_rows,
    value_rows,
    doc_lengths,
    gate_input,
    bc_input,
    step_size,
    decay_rate,
    skip_gain,
    conv_x,
    conv_bc,
    norm_gain,
):
    ctx = lax.axis_index("ctx")
    tp = lax.axis_index("tp")
    near = ctx % NEAR
    core = tp % 2
    group = tp // 2
    info = jnp.stack([(ctx // NEAR) * ROW, near, core, ctx * SHARD]).astype(jnp.int32)

    bc_mine = lax.dynamic_slice(bc_input, (0, core, group, 0), (SHARD, 1, 1, STATE)).reshape(
        SHARD, STATE
    )
    taps_mine = lax.dynamic_slice(conv_bc, (0, core, group, 0), (4, 1, 1, STATE)).reshape(4, STATE)
    rim = from_shard_behind(jnp.concatenate([queries[SHARD - RIM :], bc_mine[SHARD - RIM :]], 1))
    own = exchange_near(
        call(
            pair_kernel,
            [((NEAR, SHARD, 2 * HEAD), BF16)],
            (key_rows, value_rows),
            raw=(0, 1),
            raw_out=True,
            scratch=[pltpu.SemaphoreType.DMA((2 * NEAR,))],
        ).reshape(ROW, 2 * HEAD)
    )
    packed = call(
        pack_kernel,
        [((NEAR, PACK_ROWS, HEAD), BF16)],
        (info, doc_lengths, queries, step_size, bc_mine, rim, taps_mine),
        smem=2,
        scratch=[pltpu.VMEM((RIM + SHARD, STATE), F32)],
    )
    own, packed = lax.optimization_barrier((own, packed))
    half = ROW // 2
    back1 = from_row_behind(own, 1)
    back2a = from_row_behind(own[:half], 2)
    back2b = from_row_behind(own[half:], 2)
    back3 = from_row_behind(own[half:], 3)
    received = exchange_near(packed.reshape(NEAR * PACK_ROWS, HEAD)).reshape(
        NEAR, PACK_ROWS, HEAD
    )
    weigh, decays, since, seen = call(
        weights_kernel,
        [((ROW, HEAD), F32), ((16, STATE), F32), ((ROW, HEAD), F32), ((ROW, HEAD), F32)],
        (info, doc_lengths, decay_rate, received),
        smem=3,
    )
    received, weigh, back1, back2a, back2b, back3 = lax.optimization_barrier(
        (received, weigh, back1, back2a, back2b, back3)
    )
    other = with_partner(received[:, BC_AT:])
    attended = run_attend(info, doc_lengths, received, own, back1, back2a, back2b, back3, seen)
    x, states, handed = run_scan(info, attended, received, other, conv_x, weigh, decays, since)
    handed = lax.all_to_all(
        handed.reshape(FAR * (HEAD + 16), STATE),
        "ctx",
        0,
        0,
        axis_index_groups=far_groups(),
        tiled=True,
    ).reshape(FAR, HEAD + 16, STATE)
    y_inner, enter_row, c_row = call(
        inner_kernel,
        [((ROW, HEAD), F32), ((ROW, HEAD), F32), ((ROW, STATE), BF16)],
        (info, doc_lengths, decay_rate, skip_gain, received, other, x, states),
        smem=4,
        flops=1 << 30,
    )
    y_row = call(
        carried_kernel,
        [((ROW, HEAD), BF16)],
        (info, y_inner, enter_row, c_row, handed),
        smem=1,
    )
    y_heads = exchange_near(y_row).reshape(NEAR, SHARD, HEAD)
    sums = call(square_kernel, [((SHARD, HEAD), F32)], (y_heads, gate_input))
    partner = with_partner(sums)
    return call(
        norm_kernel,
        [((SHARD, NEAR * HEAD), BF16)],
        (y_heads, gate_input, sums, partner, norm_gain.reshape(1, -1)),
    )


def solution(mesh):
    return jax.shard_map(
        on_device,
        mesh=mesh,
        in_specs=(
            P("ctx", "tp"),
            P("ctx", "tp"),
            P("ctx", "tp"),
            P(),
            P("ctx", "tp"),
            P("ctx", None, None, None),
            P("ctx", "tp"),
            P("tp"),
            P("tp"),
            P(None, "tp"),
            P(),
            P("tp"),
        ),
        out_specs=P("ctx", "tp"),
        check_vma=False,
    )
```

```python
import math

import jax
import jax.numpy as jnp
from jax import lax
from jax.experimental import pallas as pl
from jax.experimental.pallas import tpu as pltpu
from jax.sharding import PartitionSpec as P

EPSILON = 1e-05
NEGATIVE_FILL = -1e30
NEAR = 8
FAR = 4
SHARD = 128
ROW = NEAR * SHARD
CHUNK = 256
CHUNKS = ROW // CHUNK
HEAD = 128
STATE = 256
RIM = 16
DOCS_AT = 4
PAST = 10 * CHUNK
WIDE = 256
STEPS_AT = SHARD + RIM
BC_AT = STEPS_AT + 16
PACK_ROWS = BC_AT + 2 * SHARD
EXP2_SCALE = math.log2(math.e) / math.sqrt(HEAD)
F32 = jnp.float32
BF16 = jnp.bfloat16


def near_groups():
    return [[x * NEAR + z for z in range(NEAR)] for x in range(FAR)]


def far_groups():
    return [[x * NEAR + z for x in range(FAR)] for z in range(NEAR)]


def exchange_near(x):
    return lax.all_to_all(x, "ctx", 0, 0, axis_index_groups=near_groups(), tiled=True)


def from_row_behind(x, by):
    pairs = [(x0 * NEAR + z, (x0 + by) * NEAR + z) for x0 in range(FAR - by) for z in range(NEAR)]
    return lax.ppermute(x, "ctx", pairs)


def from_shard_behind(x):
    return lax.ppermute(x, "ctx", [(i, i + 1) for i in range(NEAR * FAR - 1)])


def with_partner(x):
    count = lax.axis_size("tp")
    return lax.ppermute(x, "tp", [(t, t ^ 1) for t in range(count)])


def first_tokens(info, pos):
    begin = jnp.int32(0)
    first = pos
    for d in range(DOCS_AT, info.shape[0]):
        first = jnp.where(pos >= begin, begin, first)
        begin = begin + info[d]
    return first


def columns_of(rows):
    count = rows[0].shape[1]
    rows = list(rows) + [jnp.zeros((1, count), F32)] * (8 - len(rows))
    return jnp.transpose(jnp.concatenate(rows, 0))


def silu(v):
    return v / (1.0 + jnp.exp(-v))


def pack_kernel(info, queries, steps, raw, rim, taps, out, ext):
    ext[0:RIM] = rim[:, NEAR * HEAD :].astype(F32)
    ext[RIM:] = raw[...].astype(F32)
    pos = info[3] + lax.broadcasted_iota(jnp.int32, (1, SHARD), 1)
    since = columns_of([(pos - first_tokens(info, pos)).astype(F32)])[:, 0:1]
    acc = jnp.zeros((SHARD, STATE), F32)
    for m in range(4):
        part = ext[RIM - m : RIM - m + SHARD] * taps[3 - m : 4 - m]
        acc = acc + jnp.where(since >= m, part, 0.0)
    convolved = silu(acc).astype(BF16)
    wide = jnp.concatenate([steps[...], jnp.zeros((SHARD, HEAD - 2 * NEAR), F32)], 1)
    rows = jnp.transpose(wide)
    high = rows.astype(BF16).astype(F32)
    middle = (rows - high).astype(BF16).astype(F32)
    low = rows - high - middle
    for n in range(NEAR):
        out[n, 0:SHARD] = queries[:, n * HEAD : (n + 1) * HEAD]
        two = slice(2 * n, 2 * n + 2)
        out[n, SHARD:STEPS_AT] = rim[:, n * HEAD : (n + 1) * HEAD]
        out[n, STEPS_AT:BC_AT] = jnp.concatenate(
            [high[two], middle[two], low[two], jnp.zeros((10, HEAD), F32)], 0
        ).astype(BF16)
        out[n, BC_AT : BC_AT + SHARD] = convolved[:, 0:HEAD]
        out[n, BC_AT + SHARD :] = convolved[:, HEAD:]


def two_heads(first, second, shape):
    lane = lax.broadcasted_iota(jnp.int32, shape, 1)
    return jnp.where(lane < HEAD // 2, jnp.broadcast_to(first, shape), jnp.broadcast_to(second, shape))


def steps_of(received):
    pieces = []
    for s in range(NEAR):
        piece = received[s, STEPS_AT:BC_AT].astype(F32)
        pieces.append(piece[0:2] + piece[2:4] + piece[4:6])
    return jnp.concatenate(pieces, 1)


def decays_of(steps, rates, near):
    rate = jnp.concatenate(
        [jnp.full((1, ROW), rates[2 * near], F32), jnp.full((1, ROW), rates[2 * near + 1], F32)], 0
    )
    log_decay = -rate * steps
    stacked = jnp.concatenate(
        [log_decay[:, k * CHUNK : (k + 1) * CHUNK] for k in range(CHUNKS)], 0
    )
    high = stacked.astype(BF16)
    rest = stacked - high.astype(F32)
    middle = rest.astype(BF16)
    low = (rest - middle.astype(F32)).astype(BF16)
    below = lax.broadcasted_iota(jnp.int32, (CHUNK, CHUNK), 0)
    across = lax.broadcasted_iota(jnp.int32, (CHUNK, CHUNK), 1)
    upper = jnp.where(below <= across, 1.0, 0.0).astype(BF16)
    summed = jnp.dot(
        jnp.concatenate([high, middle, low, jnp.zeros_like(high)], 0),
        upper,
        preferred_element_type=F32,
    )
    summed = summed[0:8] + (summed[8:16] + summed[16:24])
    locals_ = [summed[2 * k : 2 * k + 2] for k in range(CHUNKS)]
    return locals_, [local[:, CHUNK - 1 : CHUNK] for local in locals_]


def places_kernel(info, since, seen):
    row_start = info[0]
    pos = row_start + lax.broadcasted_iota(jnp.int32, (1, ROW), 1)
    first = first_tokens(info, pos)
    columns = columns_of([(pos - first).astype(F32), (first - row_start).astype(F32)])
    since[...] = jnp.broadcast_to(columns[:, 0:1], (ROW, HEAD))
    seen[...] = jnp.broadcast_to(columns[:, 1:2], (ROW, HEAD))


def weights_kernel(info, rates, received, weigh, decays):
    steps = steps_of(received)
    locals_, totals = decays_of(steps, rates, info[1])
    row_start = info[0]
    pos = row_start + lax.broadcasted_iota(jnp.int32, (1, ROW), 1)
    first = first_tokens(info, pos)
    rows_, decay_rows = [], []
    for k in range(CHUNKS):
        rows = slice(k * CHUNK, (k + 1) * CHUNK)
        last_start = first[:, (k + 1) * CHUNK - 1 : (k + 1) * CHUNK]
        gap = jnp.where(pos[:, rows] >= last_start, totals[k] - locals_[k], NEGATIVE_FILL)
        rows_.append(jnp.exp(gap) * steps[:, rows])
        crossing = jnp.where(last_start < row_start + k * CHUNK, jnp.exp(totals[k]), 0.0)
        decay_rows.append(jnp.broadcast_to(crossing, (2, STATE)))
    w = jnp.concatenate(rows_, 1)
    columns = columns_of([w[0:1], w[1:2]])
    weigh[...] = two_heads(columns[:, 0:1], columns[:, 1:2], (ROW, HEAD))
    whole = totals[0] + totals[1] + totals[2] + totals[3]
    last = jnp.where(first[:, ROW - 1 : ROW] < row_start, jnp.exp(whole), 0.0)
    decay_rows.append(jnp.broadcast_to(last, (2, STATE)))
    decays[...] = jnp.concatenate(decay_rows + [jnp.zeros((6, STATE), F32)], 0)


def two_head_rows(pair):
    shape = (HEAD, STATE)
    channel = lax.broadcasted_iota(jnp.int32, shape, 0)
    return jnp.where(
        channel < HEAD // 2,
        jnp.broadcast_to(pair[0:1], shape),
        jnp.broadcast_to(pair[1:2], shape),
    )


def dot_rows(left, right):
    return lax.dot_general(left, right, (((1,), (1,)), ((), ())), preferred_element_type=F32)


def chunk_of(choose_mine, received, other, k):
    halves = []
    two = slice(2 * k, 2 * k + 2)
    for half in range(2):
        mine = received[two, BC_AT + half * SHARD : BC_AT + (half + 1) * SHARD]
        theirs = other[two, half * SHARD : (half + 1) * SHARD]
        halves.append(jnp.where(choose_mine, mine, theirs))
    return jnp.concatenate([half.reshape(CHUNK, HEAD) for half in halves], 1)


def masked(raw, offset, seen_rows, diagonal):
    count = raw.shape[0]
    slabs = []
    for n in range(raw.shape[1] // HEAD):
        place = lax.broadcasted_iota(jnp.int32, (1, HEAD), 1) + (offset + n * HEAD)
        visible = place.astype(F32) >= seen_rows
        if diagonal is not None:
            down = lax.broadcasted_iota(jnp.int32, (count, HEAD), 0) + diagonal
            along = lax.broadcasted_iota(jnp.int32, (count, HEAD), 1) + n * HEAD
            visible = visible & (along <= down)
        slabs.append(jnp.where(visible, raw[:, n * HEAD : (n + 1) * HEAD], NEGATIVE_FILL))
    return slabs


def largest_of(slabs):
    most = slabs[0]
    for slab in slabs[1:]:
        most = jnp.maximum(most, slab)
    return jnp.max(most, axis=1, keepdims=True)


def weighed(slabs, new_top):
    parts, sums = [], None
    for slab in slabs:
        weight = jnp.exp2((slab - new_top) * EXP2_SCALE)
        sums = weight if sums is None else sums + weight
        parts.append(weight.astype(BF16))
    return sums, parts


def attend_own_kernel(received, own, seen, top, total, summed):
    raws, weights = [], [[] for _ in range(CHUNKS)]
    for j in range(CHUNKS):
        query = received[2 * j :, 0:SHARD, :].reshape(ROW - j * CHUNK, HEAD)
        at = slice(j * CHUNK, (j + 1) * CHUNK)
        raws.append(dot_rows(query, own[at, 0:HEAD]))
    for i in range(CHUNKS):
        rows = slice(i * CHUNK, (i + 1) * CHUNK)
        slabs = []
        for j in range(i + 1):
            raw = raws[j][(i - j) * CHUNK : (i - j + 1) * CHUNK]
            slabs += masked(raw, j * CHUNK, seen[rows], 0 if i == j else None)
        first_top = jnp.broadcast_to(largest_of(slabs), (CHUNK, HEAD))
        sums, parts = weighed(slabs, first_top)
        top[rows] = first_top
        total[rows] = sums
        for j in range(i + 1):
            weights[j].append(jnp.concatenate(parts[2 * j : 2 * j + 2], 1))
    for j in range(CHUNKS):
        values = own[j * CHUNK : (j + 1) * CHUNK, HEAD:]
        product = jnp.dot(jnp.concatenate(weights[j], 0), values, preferred_element_type=F32)
        rows = slice(j * CHUNK, ROW)
        summed[rows] = product if j == 0 else summed[rows] + product


def attend_kernel(
    info,
    received,
    back1,
    back2,
    back3,
    seen,
    top_in,
    total_in,
    summed_in,
    attended,
    top,
    total,
    summed,
    halo_seen,
    halo_top,
    halo_total,
    halo_summed,
):
    row_start = info[0]
    halo_pos = row_start - RIM + lax.broadcasted_iota(jnp.int32, (1, HEAD), 1)
    halo_first = columns_of([(first_tokens(info, halo_pos) - row_start).astype(F32)])
    halo_seen[...] = jnp.broadcast_to(halo_first[0:RIM, 0:1], (RIM, HEAD))
    begin = jnp.int32(0)
    cross_start, cross_end = jnp.int32(0), jnp.int32(0)
    for d in range(DOCS_AT, info.shape[0]):
        inside = begin <= row_start
        cross_start = jnp.where(inside, begin, cross_start)
        begin = begin + info[d]
        cross_end = jnp.where(inside, begin, cross_end)
    reached = cross_end - row_start
    wide_blocks = PAST // WIDE
    lowest = lax.div(cross_start - row_start + PAST, jnp.int32(WIDE))

    def fold(query, keys, block, within, seen_ref, top_ref, total_ref, summed_ref, rows, diagonal):
        at = pl.ds(pl.multiple_of(within * WIDE, WIDE), WIDE)
        raw = dot_rows(query, keys[at, 0:HEAD])
        slabs = masked(raw, block * WIDE - PAST, seen_ref[rows], diagonal)
        old_top = top_ref[rows]
        new_top = jnp.maximum(old_top, largest_of(slabs))
        factor = jnp.exp2((old_top - new_top) * EXP2_SCALE)
        sums, parts = weighed(slabs, new_top)
        product = jnp.dot(
            jnp.concatenate(parts, 1), keys[at, HEAD:], preferred_element_type=F32
        )
        top_ref[rows] = new_top
        total_ref[rows] = total_ref[rows] * factor + sums
        summed_ref[rows] = summed_ref[rows] * factor + product

    top[...] = top_in[...]
    total[...] = total_in[...]
    summed[...] = summed_in[...]
    halo_top[...] = jnp.full((RIM, HEAD), NEGATIVE_FILL, F32)
    halo_total[...] = jnp.zeros((RIM, HEAD), F32)
    halo_summed[...] = jnp.zeros((RIM, HEAD), F32)

    def earlier(count):
        query = received[0 : 2 * count, 0:SHARD, :].reshape(count * CHUNK, HEAD)
        for keys, begin in ((back1, 6), (back2, 2), (back3, 0)):
            blocks = keys.shape[0] // WIDE

            def visit(n, carry):
                within = blocks - 1 - n
                block = begin + within
                fold(
                    query, keys, block, within, seen, top, total, summed, slice(0, count * CHUNK), None
                )
                fold(
                    received[0, SHARD:STEPS_AT],
                    keys,
                    block,
                    within,
                    halo_seen,
                    halo_top,
                    halo_total,
                    halo_summed,
                    slice(0, RIM),
                    (PAST - RIM) - block * WIDE,
                )
                return carry

            lax.fori_loop(0, jnp.clip(begin + blocks - lowest, 0, blocks), visit, 0)

    @pl.when(reached <= CHUNK)
    def _():
        earlier(1)

    @pl.when((reached > CHUNK) & (reached <= 2 * CHUNK))
    def _():
        earlier(2)

    @pl.when(reached > 2 * CHUNK)
    def _():
        earlier(CHUNKS)

    def finish(total_ref, summed_ref):
        whole = jnp.sum(total_ref[...], axis=1, keepdims=True)
        return (summed_ref[...] / jnp.maximum(whole, 0.5)).astype(BF16)

    attended[0:RIM] = finish(halo_total, halo_summed)
    attended[RIM:] = finish(total, summed)


def scan_kernel(
    info, attended, received, other, taps, weigh, decays, since, x_out, states, handed, ext
):
    ext[...] = attended[...].astype(F32)
    near = info[1]
    own_taps = taps[:, pl.ds(pl.multiple_of(near * HEAD, HEAD), HEAD)]
    core_zero = info[2] == 0
    state = jnp.zeros((HEAD, STATE), F32)
    for k in range(CHUNKS):
        rows = slice(k * CHUNK, (k + 1) * CHUNK)
        acc = jnp.zeros((CHUNK, HEAD), F32)
        for m in range(4):
            part = ext[RIM - m + k * CHUNK : RIM - m + (k + 1) * CHUNK] * own_taps[3 - m : 4 - m]
            acc = acc + jnp.where(since[rows] >= m, part, 0.0)
        x = silu(acc).astype(BF16)
        x_out[rows] = x
        states[k] = state.astype(BF16)
        weighed = (x.astype(F32) * weigh[rows]).astype(BF16)
        added = lax.dot_general(
            weighed,
            chunk_of(core_zero, received, other, k),
            (((0,), (0,)), ((), ())),
            preferred_element_type=F32,
        )
        state = state * two_head_rows(decays[2 * k : 2 * k + 2]) + added
    decay = decays[2 * CHUNKS : 2 * CHUNKS + 2]
    high = decay.astype(BF16).astype(F32)
    tail = jnp.concatenate([high, decay - high, jnp.zeros((12, STATE), F32)], 0).astype(BF16)
    state = state.astype(BF16)
    for r in range(FAR):
        handed[r, 0:HEAD] = state
        handed[r, HEAD:] = tail


def inner_kernel(
    info, rates, received, other, x_in, states, y_out, enter_row, c_out
):
    near = info[1]
    core_zero = info[2] == 0
    steps = steps_of(received)
    locals_, totals = decays_of(steps, rates, near)
    row_start = info[0]
    pos = row_start + lax.broadcasted_iota(jnp.int32, (1, ROW), 1)
    first = first_tokens(info, pos)
    below = lax.broadcasted_iota(jnp.int32, (CHUNK, CHUNK), 0)
    across = lax.broadcasted_iota(jnp.int32, (CHUNK, CHUNK), 1)
    causal = across <= below
    place = across.astype(F32)
    gains_at = 2 * NEAR + 2 * near
    gain = two_heads(rates[gains_at], rates[gains_at + 1], (1, HEAD))
    shape = (CHUNK, HEAD)
    before = jnp.zeros((2, 1), F32)
    for k in range(CHUNKS):
        rows = slice(k * CHUNK, (k + 1) * CHUNK)
        chunk_start = row_start + k * CHUNK
        local = locals_[k]
        e_chunk = jnp.exp(jnp.where(first[:, rows] < chunk_start, local, NEGATIVE_FILL))
        e_row = jnp.exp(jnp.where(first[:, rows] < row_start, before + local, NEGATIVE_FILL))
        before = before + totals[k]
        columns = jnp.transpose(jnp.concatenate([e_chunk, e_row, local, jnp.zeros((2, CHUNK), F32)], 0))
        since = columns_of([(first[:, rows] - chunk_start).astype(F32)])[:, 0:1]
        enter_row[rows] = two_heads(columns[:, 2:3], columns[:, 3:4], shape)
        c_values = chunk_of(jnp.logical_not(core_zero), received, other, k)
        c_out[rows] = c_values
        gram = dot_rows(c_values, chunk_of(core_zero, received, other, k))
        visible = causal & (place >= since)
        x = x_in[rows]
        halves = []
        for h in range(2):
            gap = jnp.where(visible, columns[:, 4 + h : 5 + h] - local[h : h + 1], NEGATIVE_FILL)
            mix = (gram * jnp.exp(gap) * steps[h : h + 1, rows]).astype(BF16)
            halves.append(jnp.dot(mix, x, preferred_element_type=F32))
        lane = lax.broadcasted_iota(jnp.int32, shape, 1)
        y = jnp.where(lane < HEAD // 2, halves[0], halves[1]) + x.astype(F32) * gain
        if k > 0:
            carried = dot_rows(c_values, states[k])
            y = y + two_heads(columns[:, 0:1], columns[:, 1:2], shape) * carried
        y_out[rows] = y


def carried_kernel(info, y_in, enter_row, c_in, handed, y_out):
    entering = jnp.zeros((HEAD, STATE), F32)
    for r in range(FAR - 1):
        tail = handed[r, HEAD:].astype(F32)
        decay = two_head_rows(tail[0:2] + tail[2:4])
        following = entering * decay + handed[r, 0:HEAD].astype(F32)
        entering = jnp.where(r * ROW < info[0], following, entering)
    entering = entering.astype(BF16)
    for k in range(CHUNKS):
        rows = slice(k * CHUNK, (k + 1) * CHUNK)
        carried = dot_rows(c_in[rows], entering)
        y_out[rows] = (y_in[rows] + enter_row[rows] * carried).astype(BF16)


def gated_of(y, gate, h):
    return y[h].astype(F32) * silu(gate[:, h * HEAD : (h + 1) * HEAD].astype(F32))


def square_kernel(y, gate, sums):
    acc = jnp.zeros((SHARD, HEAD), F32)
    for h in range(NEAR):
        gated = gated_of(y, gate, h)
        acc = acc + gated * gated
    sums[...] = jnp.broadcast_to(jnp.sum(acc, axis=1, keepdims=True), (SHARD, HEAD))


def norm_kernel(y, gate, sums, partner, gain, out):
    mean = (sums[...] + partner[...]) / (2.0 * NEAR * HEAD)
    scale = lax.rsqrt(mean + EPSILON)
    for h in range(NEAR):
        columns = slice(h * HEAD, (h + 1) * HEAD)
        out[:, columns] = (gated_of(y, gate, h) * scale * gain[:, columns]).astype(BF16)


def call(kernel, outs, args, smem=0, raw=(), raw_out=False, scratch=(), flops=0, mib=8):
    specs = []
    for n in range(len(args)):
        if n < smem:
            specs.append(pl.BlockSpec(memory_space=pltpu.SMEM))
        elif n in raw:
            specs.append(pl.BlockSpec(memory_space=pl.ANY))
        else:
            specs.append(pl.BlockSpec(memory_space=pltpu.VMEM))
    single = len(outs) == 1
    shapes = [jax.ShapeDtypeStruct(shape, kind) for shape, kind in outs]
    out_specs = [pl.BlockSpec(memory_space=pl.ANY if raw_out else pltpu.VMEM)] * len(outs)
    return pl.pallas_call(
        kernel,
        out_shape=shapes[0] if single else shapes,
        in_specs=specs,
        out_specs=out_specs[0] if single else out_specs,
        scratch_shapes=list(scratch),
        compiler_params=pltpu.CompilerParams(vmem_limit_bytes=mib * 1024 * 1024),
        cost_estimate=pl.CostEstimate(flops=flops, bytes_accessed=1 << 21, transcendentals=0),
    )(*args)


def run_attend(info, received, *args):
    return call(
        attend_kernel,
        [((RIM + ROW, HEAD), BF16)],
        (info, received, *args),
        smem=1,
        scratch=[
            pltpu.VMEM((ROW, HEAD), F32),
            pltpu.VMEM((ROW, HEAD), F32),
            pltpu.VMEM((ROW, HEAD), F32),
            pltpu.VMEM((RIM, HEAD), F32),
            pltpu.VMEM((RIM, HEAD), F32),
            pltpu.VMEM((RIM, HEAD), F32),
            pltpu.VMEM((RIM, HEAD), F32),
        ],
        flops=1 << 32,
        mib=12,
    )


def run_scan(info, attended, received, other, taps, weigh, decays, since):
    return call(
        scan_kernel,
        [
            ((ROW, HEAD), BF16),
            ((CHUNKS, HEAD, STATE), BF16),
            ((FAR, HEAD + 16, STATE), BF16),
        ],
        (info, attended, received, other, taps, weigh, decays, since),
        smem=1,
        scratch=[pltpu.VMEM((RIM + ROW, HEAD), F32)],
    )


def on_device(
    queries,
    key_rows,
    value_rows,
    doc_lengths,
    gate_input,
    bc_input,
    step_size,
    decay_rate,
    skip_gain,
    conv_x,
    conv_bc,
    norm_gain,
):
    ctx = lax.axis_index("ctx")
    tp = lax.axis_index("tp")
    near = ctx % NEAR
    core = tp % 2
    group = tp // 2
    place = jnp.stack([(ctx // NEAR) * ROW, near, core, ctx * SHARD]).astype(jnp.int32)
    info = jnp.concatenate([place, doc_lengths])
    rates = jnp.concatenate([decay_rate, skip_gain])

    bc_mine = lax.dynamic_slice(bc_input, (0, core, group, 0), (SHARD, 1, 1, STATE)).reshape(
        SHARD, STATE
    )
    taps_mine = lax.dynamic_slice(conv_bc, (0, core, group, 0), (4, 1, 1, STATE)).reshape(4, STATE)
    rim = from_shard_behind(jnp.concatenate([queries[SHARD - RIM :], bc_mine[SHARD - RIM :]], 1))
    wide = (NEAR, SHARD, HEAD)
    pairs = jnp.concatenate(
        [jnp.broadcast_to(key_rows, wide), jnp.broadcast_to(value_rows, wide)], 2
    )
    own = exchange_near(pairs.reshape(ROW, 2 * HEAD))
    since, seen = call(places_kernel, [((ROW, HEAD), F32)] * 2, (info,), smem=1)
    packed = call(
        pack_kernel,
        [((NEAR, PACK_ROWS, HEAD), BF16)],
        (info, queries, step_size, bc_mine, rim, taps_mine),
        smem=1,
        scratch=[pltpu.VMEM((RIM + SHARD, STATE), F32)],
    )
    own, packed = lax.optimization_barrier((own, packed))
    half = ROW // 2
    back1 = from_row_behind(own, 1)
    back2 = from_row_behind(own, 2)
    back3 = from_row_behind(own[half:], 3)
    received = exchange_near(packed.reshape(NEAR * PACK_ROWS, HEAD)).reshape(
        NEAR, PACK_ROWS, HEAD
    )
    weigh, decays = call(
        weights_kernel,
        [((ROW, HEAD), F32), ((16, STATE), F32)],
        (info, rates, received),
        smem=2,
    )
    own_part = call(attend_own_kernel, [((ROW, HEAD), F32)] * 3, (received, own, seen), mib=12)
    received, weigh, back1, back2, back3, *own_part = lax.optimization_barrier(
        (received, weigh, back1, back2, back3, *own_part)
    )
    other = with_partner(received[:, BC_AT:])
    attended = run_attend(info, received, back1, back2, back3, seen, *own_part)
    x, states, handed = run_scan(info, attended, received, other, conv_x, weigh, decays, since)
    handed = lax.all_to_all(
        handed.reshape(FAR * (HEAD + 16), STATE),
        "ctx",
        0,
        0,
        axis_index_groups=far_groups(),
        tiled=True,
    ).reshape(FAR, HEAD + 16, STATE)
    y_inner, enter_row, c_row = call(
        inner_kernel,
        [((ROW, HEAD), F32), ((ROW, HEAD), F32), ((ROW, STATE), BF16)],
        (info, rates, received, other, x, states),
        smem=2,
        flops=1 << 30,
    )
    y_row = call(
        carried_kernel,
        [((ROW, HEAD), BF16)],
        (info, y_inner, enter_row, c_row, handed),
        smem=1,
    )
    y_heads = exchange_near(y_row).reshape(NEAR, SHARD, HEAD)
    sums = call(square_kernel, [((SHARD, HEAD), F32)], (y_heads, gate_input))
    partner = with_partner(sums)
    return call(
        norm_kernel,
        [((SHARD, NEAR * HEAD), BF16)],
        (y_heads, gate_input, sums, partner, norm_gain.reshape(1, -1)),
    )


def solution(mesh):
    return jax.shard_map(
        on_device,
        mesh=mesh,
        in_specs=(
            P("ctx", "tp"),
            P("ctx", "tp"),
            P("ctx", "tp"),
            P(),
            P("ctx", "tp"),
            P("ctx", None, None, None),
            P("ctx", "tp"),
            P("tp"),
            P("tp"),
            P(None, "tp"),
            P(),
            P("tp"),
        ),
        out_specs=P("ctx", "tp"),
        check_vma=False,
    )
```

```python
import math

import jax
import jax.numpy as jnp
from jax import lax
from jax.experimental import pallas as pl
from jax.experimental.pallas import tpu as pltpu
from jax.sharding import PartitionSpec as P

EPSILON = 1e-05
NEGATIVE_FILL = -1e30
NEAR = 8
FAR = 4
SHARD = 128
ROW = NEAR * SHARD
CHUNK = 256
CHUNKS = ROW // CHUNK
HEAD = 128
STATE = 256
RIM = 16
DOCS_AT = 4
PAST = 10 * CHUNK
WIDE = 256
STEPS_AT = SHARD + RIM
BC_AT = STEPS_AT + 16
PACK_ROWS = BC_AT + 2 * SHARD
EXP2_SCALE = math.log2(math.e) / math.sqrt(HEAD)
F32 = jnp.float32
BF16 = jnp.bfloat16


def near_groups():
    return [[x * NEAR + z for z in range(NEAR)] for x in range(FAR)]


def far_groups():
    return [[x * NEAR + z for x in range(FAR)] for z in range(NEAR)]


def exchange_near(x):
    return lax.all_to_all(x, "ctx", 0, 0, axis_index_groups=near_groups(), tiled=True)


def from_row_behind(x, by):
    pairs = [(x0 * NEAR + z, (x0 + by) * NEAR + z) for x0 in range(FAR - by) for z in range(NEAR)]
    return lax.ppermute(x, "ctx", pairs)


def from_shard_behind(x):
    return lax.ppermute(x, "ctx", [(i, i + 1) for i in range(NEAR * FAR - 1)])


def with_partner(x):
    count = lax.axis_size("tp")
    return lax.ppermute(x, "tp", [(t, t ^ 1) for t in range(count)])


def first_tokens(info, pos):
    begin = jnp.int32(0)
    first = pos
    for d in range(DOCS_AT, info.shape[0]):
        first = jnp.where(pos >= begin, begin, first)
        begin = begin + info[d]
    return first


def columns_of(rows):
    count = rows[0].shape[1]
    rows = list(rows) + [jnp.zeros((1, count), F32)] * (8 - len(rows))
    return jnp.transpose(jnp.concatenate(rows, 0))


def silu(v):
    return v / (1.0 + jnp.exp(-v))


def pack_kernel(info, queries, steps, raw, rim, taps, out, ext):
    ext[0:RIM] = rim[:, NEAR * HEAD :].astype(F32)
    ext[RIM:] = raw[...].astype(F32)
    pos = info[3] + lax.broadcasted_iota(jnp.int32, (1, SHARD), 1)
    since = columns_of([(pos - first_tokens(info, pos)).astype(F32)])[:, 0:1]
    acc = jnp.zeros((SHARD, STATE), F32)
    for m in range(4):
        part = ext[RIM - m : RIM - m + SHARD] * taps[3 - m : 4 - m]
        acc = acc + jnp.where(since >= m, part, 0.0)
    convolved = silu(acc).astype(BF16)
    wide = jnp.concatenate([steps[...], jnp.zeros((SHARD, HEAD - 2 * NEAR), F32)], 1)
    rows = jnp.transpose(wide)
    high = rows.astype(BF16).astype(F32)
    middle = (rows - high).astype(BF16).astype(F32)
    low = rows - high - middle
    for n in range(NEAR):
        out[n, 0:SHARD] = queries[:, n * HEAD : (n + 1) * HEAD]
        two = slice(2 * n, 2 * n + 2)
        out[n, SHARD:STEPS_AT] = rim[:, n * HEAD : (n + 1) * HEAD]
        out[n, STEPS_AT:BC_AT] = jnp.concatenate(
            [high[two], middle[two], low[two], jnp.zeros((10, HEAD), F32)], 0
        ).astype(BF16)
        out[n, BC_AT : BC_AT + SHARD] = convolved[:, 0:HEAD]
        out[n, BC_AT + SHARD :] = convolved[:, HEAD:]


def two_heads(first, second, shape):
    lane = lax.broadcasted_iota(jnp.int32, shape, 1)
    return jnp.where(lane < HEAD // 2, jnp.broadcast_to(first, shape), jnp.broadcast_to(second, shape))


def steps_of(received):
    pieces = []
    for s in range(NEAR):
        piece = received[s, STEPS_AT:BC_AT].astype(F32)
        pieces.append(piece[0:2] + piece[2:4] + piece[4:6])
    return jnp.concatenate(pieces, 1)


def decays_of(steps, rates, near):
    rate = jnp.concatenate(
        [jnp.full((1, ROW), rates[2 * near], F32), jnp.full((1, ROW), rates[2 * near + 1], F32)], 0
    )
    log_decay = -rate * steps
    stacked = jnp.concatenate(
        [log_decay[:, k * CHUNK : (k + 1) * CHUNK] for k in range(CHUNKS)], 0
    )
    high = stacked.astype(BF16)
    rest = stacked - high.astype(F32)
    middle = rest.astype(BF16)
    low = (rest - middle.astype(F32)).astype(BF16)
    below = lax.broadcasted_iota(jnp.int32, (CHUNK, CHUNK), 0)
    across = lax.broadcasted_iota(jnp.int32, (CHUNK, CHUNK), 1)
    upper = jnp.where(below <= across, 1.0, 0.0).astype(BF16)
    summed = jnp.dot(
        jnp.concatenate([high, middle, low, jnp.zeros_like(high)], 0),
        upper,
        preferred_element_type=F32,
    )
    summed = summed[0:8] + (summed[8:16] + summed[16:24])
    locals_ = [summed[2 * k : 2 * k + 2] for k in range(CHUNKS)]
    return locals_, [local[:, CHUNK - 1 : CHUNK] for local in locals_]


def places_kernel(info, seen):
    row_start = info[0]
    pos = row_start + lax.broadcasted_iota(jnp.int32, (1, ROW), 1)
    first = first_tokens(info, pos)
    columns = columns_of([(first - row_start).astype(F32)])
    seen[...] = jnp.broadcast_to(columns[:, 0:1], (ROW, HEAD))


def chunk_weights(steps, local, total, pos, last_start, chunk_start):
    gap = jnp.where(pos >= last_start, total - local, NEGATIVE_FILL)
    crossing = jnp.where(last_start < chunk_start, jnp.exp(total), 0.0)
    return jnp.exp(gap) * steps, jnp.broadcast_to(crossing, (2, STATE))


def weights_kernel(info, rates, received, weigh, decays):
    steps = steps_of(received)
    locals_, totals = decays_of(steps, rates, info[1])
    row_start = info[0]
    pos = row_start + lax.broadcasted_iota(jnp.int32, (1, ROW), 1)
    first = first_tokens(info, pos)
    rows_, decay_rows = [], []
    for k in range(CHUNKS):
        rows = slice(k * CHUNK, (k + 1) * CHUNK)
        last_start = first[:, (k + 1) * CHUNK - 1 : (k + 1) * CHUNK]
        w, decay = chunk_weights(
            steps[:, rows], locals_[k], totals[k], pos[:, rows], last_start, row_start + k * CHUNK
        )
        rows_.append(w)
        decay_rows.append(decay)
    w = jnp.concatenate(rows_, 1)
    columns = columns_of([w[0:1], w[1:2]])
    weigh[...] = two_heads(columns[:, 0:1], columns[:, 1:2], (ROW, HEAD))
    whole = totals[0] + totals[1] + totals[2] + totals[3]
    last = jnp.where(first[:, ROW - 1 : ROW] < row_start, jnp.exp(whole), 0.0)
    decay_rows.append(jnp.broadcast_to(last, (2, STATE)))
    decays[...] = jnp.concatenate(decay_rows + [jnp.zeros((6, STATE), F32)], 0)


def two_head_rows(pair):
    shape = (HEAD, STATE)
    channel = lax.broadcasted_iota(jnp.int32, shape, 0)
    return jnp.where(
        channel < HEAD // 2,
        jnp.broadcast_to(pair[0:1], shape),
        jnp.broadcast_to(pair[1:2], shape),
    )


def dot_rows(left, right):
    return lax.dot_general(left, right, (((1,), (1,)), ((), ())), preferred_element_type=F32)


def chunk_of(choose_mine, received, other, k):
    halves = []
    two = slice(2 * k, 2 * k + 2)
    for half in range(2):
        mine = received[two, BC_AT + half * SHARD : BC_AT + (half + 1) * SHARD]
        theirs = other[two, half * SHARD : (half + 1) * SHARD]
        halves.append(jnp.where(choose_mine, mine, theirs))
    return jnp.concatenate([half.reshape(CHUNK, HEAD) for half in halves], 1)


def masked(raw, offset, seen_rows, diagonal):
    count = raw.shape[0]
    slabs = []
    for n in range(raw.shape[1] // HEAD):
        place = lax.broadcasted_iota(jnp.int32, (1, HEAD), 1) + (offset + n * HEAD)
        visible = place.astype(F32) >= seen_rows
        if diagonal is not None:
            down = lax.broadcasted_iota(jnp.int32, (count, HEAD), 0) + diagonal
            along = lax.broadcasted_iota(jnp.int32, (count, HEAD), 1) + n * HEAD
            visible = visible & (along <= down)
        slabs.append(jnp.where(visible, raw[:, n * HEAD : (n + 1) * HEAD], NEGATIVE_FILL))
    return slabs


def largest_of(slabs):
    most = slabs[0]
    for slab in slabs[1:]:
        most = jnp.maximum(most, slab)
    return jnp.max(most, axis=1, keepdims=True)


def weighed(slabs, new_top):
    parts, sums = [], None
    for slab in slabs:
        weight = jnp.exp2((slab - new_top) * EXP2_SCALE)
        sums = weight if sums is None else sums + weight
        parts.append(weight.astype(BF16))
    return sums, parts


def attend_own_kernel(received, own, seen, top, total, summed):
    raws, weights = [], [[] for _ in range(CHUNKS)]
    for j in range(CHUNKS):
        query = received[2 * j :, 0:SHARD, :].reshape(ROW - j * CHUNK, HEAD)
        at = slice(j * CHUNK, (j + 1) * CHUNK)
        raws.append(dot_rows(query, own[at, 0:HEAD]))
    for i in range(CHUNKS):
        rows = slice(i * CHUNK, (i + 1) * CHUNK)
        slabs = []
        for j in range(i + 1):
            raw = raws[j][(i - j) * CHUNK : (i - j + 1) * CHUNK]
            slabs += masked(raw, j * CHUNK, seen[rows], 0 if i == j else None)
        first_top = jnp.broadcast_to(largest_of(slabs), (CHUNK, HEAD))
        sums, parts = weighed(slabs, first_top)
        top[rows] = first_top
        total[rows] = sums
        for j in range(i + 1):
            weights[j].append(jnp.concatenate(parts[2 * j : 2 * j + 2], 1))
    for j in range(CHUNKS):
        values = own[j * CHUNK : (j + 1) * CHUNK, HEAD:]
        product = jnp.dot(jnp.concatenate(weights[j], 0), values, preferred_element_type=F32)
        rows = slice(j * CHUNK, ROW)
        summed[rows] = product if j == 0 else summed[rows] + product


def attend_kernel(
    info,
    received,
    back1,
    back2,
    back3,
    seen,
    top_in,
    total_in,
    summed_in,
    attended,
    top,
    total,
    summed,
    halo_seen,
    halo_top,
    halo_total,
    halo_summed,
):
    row_start = info[0]
    halo_pos = row_start - RIM + lax.broadcasted_iota(jnp.int32, (1, HEAD), 1)
    halo_first = columns_of([(first_tokens(info, halo_pos) - row_start).astype(F32)])
    halo_seen[...] = jnp.broadcast_to(halo_first[0:RIM, 0:1], (RIM, HEAD))
    begin = jnp.int32(0)
    cross_start, cross_end = jnp.int32(0), jnp.int32(0)
    for d in range(DOCS_AT, info.shape[0]):
        inside = begin <= row_start
        cross_start = jnp.where(inside, begin, cross_start)
        begin = begin + info[d]
        cross_end = jnp.where(inside, begin, cross_end)
    reached = cross_end - row_start
    wide_blocks = PAST // WIDE
    lowest = lax.div(cross_start - row_start + PAST, jnp.int32(WIDE))

    def fold(query, keys, block, within, seen_ref, top_ref, total_ref, summed_ref, rows, diagonal):
        at = pl.ds(pl.multiple_of(within * WIDE, WIDE), WIDE)
        raw = dot_rows(query, keys[at, 0:HEAD])
        slabs = masked(raw, block * WIDE - PAST, seen_ref[rows], diagonal)
        old_top = top_ref[rows]
        new_top = jnp.maximum(old_top, largest_of(slabs))
        factor = jnp.exp2((old_top - new_top) * EXP2_SCALE)
        sums, parts = weighed(slabs, new_top)
        product = jnp.dot(
            jnp.concatenate(parts, 1), keys[at, HEAD:], preferred_element_type=F32
        )
        top_ref[rows] = new_top
        total_ref[rows] = total_ref[rows] * factor + sums
        summed_ref[rows] = summed_ref[rows] * factor + product

    top[...] = top_in[...]
    total[...] = total_in[...]
    summed[...] = summed_in[...]
    halo_top[...] = jnp.full((RIM, HEAD), NEGATIVE_FILL, F32)
    halo_total[...] = jnp.zeros((RIM, HEAD), F32)
    halo_summed[...] = jnp.zeros((RIM, HEAD), F32)

    def earlier(count):
        query = received[0 : 2 * count, 0:SHARD, :].reshape(count * CHUNK, HEAD)
        for keys, begin in ((back1, 6), (back2, 2), (back3, 0)):
            blocks = keys.shape[0] // WIDE

            def visit(n, carry):
                within = blocks - 1 - n
                block = begin + within
                fold(
                    query, keys, block, within, seen, top, total, summed, slice(0, count * CHUNK), None
                )
                fold(
                    received[0, SHARD:STEPS_AT],
                    keys,
                    block,
                    within,
                    halo_seen,
                    halo_top,
                    halo_total,
                    halo_summed,
                    slice(0, RIM),
                    (PAST - RIM) - block * WIDE,
                )
                return carry

            lax.fori_loop(0, jnp.clip(begin + blocks - lowest, 0, blocks), visit, 0)

    @pl.when(reached <= CHUNK)
    def _():
        earlier(1)

    @pl.when((reached > CHUNK) & (reached <= 2 * CHUNK))
    def _():
        earlier(2)

    @pl.when(reached > 2 * CHUNK)
    def _():
        earlier(CHUNKS)

    def finish(total_ref, summed_ref):
        whole = jnp.sum(total_ref[...], axis=1, keepdims=True)
        return (summed_ref[...] / jnp.maximum(whole, 0.5)).astype(BF16)

    attended[0:RIM] = finish(halo_total, halo_summed)
    attended[RIM:] = finish(total, summed)


def scan_kernel(
    info, attended, received, other, taps, weigh, decays, seen, x_out, handed, ext
):
    ext[...] = attended[...].astype(F32)
    near = info[1]
    own_taps = taps[:, pl.ds(pl.multiple_of(near * HEAD, HEAD), HEAD)]
    core_zero = info[2] == 0
    state = jnp.zeros((HEAD, STATE), F32)
    for k in range(CHUNKS):
        rows = slice(k * CHUNK, (k + 1) * CHUNK)
        acc = jnp.zeros((CHUNK, HEAD), F32)
        place = lax.broadcasted_iota(jnp.int32, (CHUNK, HEAD), 0) + k * CHUNK
        since = place.astype(F32) - seen[rows]
        for m in range(4):
            part = ext[RIM - m + k * CHUNK : RIM - m + (k + 1) * CHUNK] * own_taps[3 - m : 4 - m]
            acc = acc + jnp.where(since >= m, part, 0.0)
        x = silu(acc).astype(BF16)
        x_out[rows] = x
        weighed = (x.astype(F32) * weigh[rows]).astype(BF16)
        added = lax.dot_general(
            weighed,
            chunk_of(core_zero, received, other, k),
            (((0,), (0,)), ((), ())),
            preferred_element_type=F32,
        )
        state = state * two_head_rows(decays[2 * k : 2 * k + 2]) + added
    decay = decays[2 * CHUNKS : 2 * CHUNKS + 2]
    high = decay.astype(BF16).astype(F32)
    tail = jnp.concatenate([high, decay - high, jnp.zeros((12, STATE), F32)], 0).astype(BF16)
    state = state.astype(BF16)
    for r in range(FAR):
        handed[r, 0:HEAD] = state
        handed[r, HEAD:] = tail


def inner_kernel(
    info, rates, received, other, x_in, y_out, enter_row, c_out
):
    near = info[1]
    core_zero = info[2] == 0
    steps = steps_of(received)
    locals_, totals = decays_of(steps, rates, near)
    row_start = info[0]
    pos = row_start + lax.broadcasted_iota(jnp.int32, (1, ROW), 1)
    first = first_tokens(info, pos)
    below = lax.broadcasted_iota(jnp.int32, (CHUNK, CHUNK), 0)
    across = lax.broadcasted_iota(jnp.int32, (CHUNK, CHUNK), 1)
    causal = across <= below
    place = across.astype(F32)
    gains_at = 2 * NEAR + 2 * near
    gain = two_heads(rates[gains_at], rates[gains_at + 1], (1, HEAD))
    shape = (CHUNK, HEAD)
    before = jnp.zeros((2, 1), F32)
    for k in range(CHUNKS):
        rows = slice(k * CHUNK, (k + 1) * CHUNK)
        chunk_start = row_start + k * CHUNK
        local = locals_[k]
        e_chunk = jnp.exp(jnp.where(first[:, rows] < chunk_start, local, NEGATIVE_FILL))
        e_row = jnp.exp(jnp.where(first[:, rows] < row_start, before + local, NEGATIVE_FILL))
        before = before + totals[k]
        last_start = first[:, (k + 1) * CHUNK - 1 : (k + 1) * CHUNK]
        w, decay = chunk_weights(
            steps[:, rows], local, totals[k], pos[:, rows], last_start, chunk_start
        )
        columns = jnp.transpose(jnp.concatenate([e_chunk, e_row, local, w], 0))
        since = columns_of([(first[:, rows] - chunk_start).astype(F32)])[:, 0:1]
        enter_row[rows] = two_heads(columns[:, 2:3], columns[:, 3:4], shape)
        c_values = chunk_of(jnp.logical_not(core_zero), received, other, k)
        c_out[rows] = c_values
        b_values = chunk_of(core_zero, received, other, k)
        gram = dot_rows(c_values, b_values)
        visible = causal & (place >= since)
        x = x_in[rows]
        halves = []
        for h in range(2):
            gap = jnp.where(visible, columns[:, 4 + h : 5 + h] - local[h : h + 1], NEGATIVE_FILL)
            mix = (gram * jnp.exp(gap) * steps[h : h + 1, rows]).astype(BF16)
            halves.append(jnp.dot(mix, x, preferred_element_type=F32))
        lane = lax.broadcasted_iota(jnp.int32, shape, 1)
        y = jnp.where(lane < HEAD // 2, halves[0], halves[1]) + x.astype(F32) * gain
        if k > 0:
            carried = dot_rows(c_values, state.astype(BF16))
            y = y + two_heads(columns[:, 0:1], columns[:, 1:2], shape) * carried
        y_out[rows] = y
        if k + 1 < CHUNKS:
            weighed = x.astype(F32) * two_heads(columns[:, 6:7], columns[:, 7:8], shape)
            added = lax.dot_general(
                weighed.astype(BF16),
                b_values,
                (((0,), (0,)), ((), ())),
                preferred_element_type=F32,
            )
            state = added if k == 0 else state * two_head_rows(decay) + added


def carried_kernel(info, y_in, enter_row, c_in, handed, y_out):
    entering = jnp.zeros((HEAD, STATE), F32)
    for r in range(FAR - 1):
        tail = handed[r, HEAD:].astype(F32)
        decay = two_head_rows(tail[0:2] + tail[2:4])
        following = entering * decay + handed[r, 0:HEAD].astype(F32)
        entering = jnp.where(r * ROW < info[0], following, entering)
    entering = entering.astype(BF16)
    for k in range(CHUNKS):
        rows = slice(k * CHUNK, (k + 1) * CHUNK)
        carried = dot_rows(c_in[rows], entering)
        y_out[rows] = (y_in[rows] + enter_row[rows] * carried).astype(BF16)


def gated_of(y, gate, h):
    return y[h].astype(F32) * silu(gate[:, h * HEAD : (h + 1) * HEAD].astype(F32))


def square_kernel(y, gate, sums):
    acc = jnp.zeros((SHARD, HEAD), F32)
    for h in range(NEAR):
        gated = gated_of(y, gate, h)
        acc = acc + gated * gated
    sums[...] = jnp.broadcast_to(jnp.sum(acc, axis=1, keepdims=True), (SHARD, HEAD))


def norm_kernel(y, gate, sums, partner, gain, out):
    mean = (sums[...] + partner[...]) / (2.0 * NEAR * HEAD)
    scale = lax.rsqrt(mean + EPSILON)
    for h in range(NEAR):
        columns = slice(h * HEAD, (h + 1) * HEAD)
        out[:, columns] = (gated_of(y, gate, h) * scale * gain[:, columns]).astype(BF16)


def call(kernel, outs, args, smem=0, raw=(), raw_out=False, scratch=(), flops=0, mib=8):
    specs = []
    for n in range(len(args)):
        if n < smem:
            specs.append(pl.BlockSpec(memory_space=pltpu.SMEM))
        elif n in raw:
            specs.append(pl.BlockSpec(memory_space=pl.ANY))
        else:
            specs.append(pl.BlockSpec(memory_space=pltpu.VMEM))
    single = len(outs) == 1
    shapes = [jax.ShapeDtypeStruct(shape, kind) for shape, kind in outs]
    out_specs = [pl.BlockSpec(memory_space=pl.ANY if raw_out else pltpu.VMEM)] * len(outs)
    return pl.pallas_call(
        kernel,
        out_shape=shapes[0] if single else shapes,
        in_specs=specs,
        out_specs=out_specs[0] if single else out_specs,
        scratch_shapes=list(scratch),
        compiler_params=pltpu.CompilerParams(vmem_limit_bytes=mib * 1024 * 1024),
        cost_estimate=pl.CostEstimate(flops=flops, bytes_accessed=1 << 21, transcendentals=0),
    )(*args)


def run_attend(info, received, *args):
    return call(
        attend_kernel,
        [((RIM + ROW, HEAD), BF16)],
        (info, received, *args),
        smem=1,
        scratch=[
            pltpu.VMEM((ROW, HEAD), F32),
            pltpu.VMEM((ROW, HEAD), F32),
            pltpu.VMEM((ROW, HEAD), F32),
            pltpu.VMEM((RIM, HEAD), F32),
            pltpu.VMEM((RIM, HEAD), F32),
            pltpu.VMEM((RIM, HEAD), F32),
            pltpu.VMEM((RIM, HEAD), F32),
        ],
        flops=1 << 32,
        mib=12,
    )


def run_scan(info, attended, received, other, taps, weigh, decays, seen):
    return call(
        scan_kernel,
        [
            ((ROW, HEAD), BF16),
            ((FAR, HEAD + 16, STATE), BF16),
        ],
        (info, attended, received, other, taps, weigh, decays, seen),
        smem=1,
        scratch=[pltpu.VMEM((RIM + ROW, HEAD), F32)],
    )


def on_device(
    queries,
    key_rows,
    value_rows,
    doc_lengths,
    gate_input,
    bc_input,
    step_size,
    decay_rate,
    skip_gain,
    conv_x,
    conv_bc,
    norm_gain,
):
    ctx = lax.axis_index("ctx")
    tp = lax.axis_index("tp")
    near = ctx % NEAR
    core = tp % 2
    group = tp // 2
    place = jnp.stack([(ctx // NEAR) * ROW, near, core, ctx * SHARD]).astype(jnp.int32)
    info = jnp.concatenate([place, doc_lengths])
    rates = jnp.concatenate([decay_rate, skip_gain])

    bc_mine = lax.dynamic_slice(bc_input, (0, core, group, 0), (SHARD, 1, 1, STATE)).reshape(
        SHARD, STATE
    )
    taps_mine = lax.dynamic_slice(conv_bc, (0, core, group, 0), (4, 1, 1, STATE)).reshape(4, STATE)
    rim = from_shard_behind(jnp.concatenate([queries[SHARD - RIM :], bc_mine[SHARD - RIM :]], 1))
    wide = (NEAR, SHARD, 2 * HEAD)
    pairs = jnp.where(
        lax.broadcasted_iota(jnp.int32, wide, 2) < HEAD,
        jnp.broadcast_to(jnp.pad(key_rows, ((0, 0), (0, HEAD))), wide),
        jnp.broadcast_to(jnp.pad(value_rows, ((0, 0), (HEAD, 0))), wide),
    )
    own = exchange_near(pairs.reshape(ROW, 2 * HEAD))
    seen = call(places_kernel, [((ROW, HEAD), F32)], (info,), smem=1)
    packed = call(
        pack_kernel,
        [((NEAR, PACK_ROWS, HEAD), BF16)],
        (info, queries, step_size, bc_mine, rim, taps_mine),
        smem=1,
        scratch=[pltpu.VMEM((RIM + SHARD, STATE), F32)],
    )
    own, packed = lax.optimization_barrier((own, packed))
    half = ROW // 2
    back1 = from_row_behind(own, 1)
    back2 = from_row_behind(own, 2)
    back3 = from_row_behind(own[half:], 3)
    received = exchange_near(packed.reshape(NEAR * PACK_ROWS, HEAD)).reshape(
        NEAR, PACK_ROWS, HEAD
    )
    weigh, decays = call(
        weights_kernel,
        [((ROW, HEAD), F32), ((16, STATE), F32)],
        (info, rates, received),
        smem=2,
    )
    own_part = call(attend_own_kernel, [((ROW, HEAD), F32)] * 3, (received, own, seen), mib=12)
    received, weigh, back1, back2, back3, *own_part = lax.optimization_barrier(
        (received, weigh, back1, back2, back3, *own_part)
    )
    other = with_partner(received[:, BC_AT:])
    attended = run_attend(info, received, back1, back2, back3, seen, *own_part)
    x, handed = run_scan(info, attended, received, other, conv_x, weigh, decays, seen)
    handed = lax.all_to_all(
        handed.reshape(FAR * (HEAD + 16), STATE),
        "ctx",
        0,
        0,
        axis_index_groups=far_groups(),
        tiled=True,
    ).reshape(FAR, HEAD + 16, STATE)
    y_inner, enter_row, c_row = call(
        inner_kernel,
        [((ROW, HEAD), F32), ((ROW, HEAD), F32), ((ROW, STATE), BF16)],
        (info, rates, received, other, x),
        smem=2,
        flops=1 << 30,
    )
    y_row = call(
        carried_kernel,
        [((ROW, HEAD), BF16)],
        (info, y_inner, enter_row, c_row, handed),
        smem=1,
    )
    y_heads = exchange_near(y_row).reshape(NEAR, SHARD, HEAD)
    sums = call(square_kernel, [((SHARD, HEAD), F32)], (y_heads, gate_input))
    partner = with_partner(sums)
    return call(
        norm_kernel,
        [((SHARD, NEAR * HEAD), BF16)],
        (y_heads, gate_input, sums, partner, norm_gain.reshape(1, -1)),
    )


def solution(mesh):
    return jax.shard_map(
        on_device,
        mesh=mesh,
        in_specs=(
            P("ctx", "tp"),
            P("ctx", "tp"),
            P("ctx", "tp"),
            P(),
            P("ctx", "tp"),
            P("ctx", None, None, None),
            P("ctx", "tp"),
            P("tp"),
            P("tp"),
            P(None, "tp"),
            P(),
            P("tp"),
        ),
        out_specs=P("ctx", "tp"),
        check_vma=False,
    )
```

```python
import math

import jax
import jax.numpy as jnp
from jax import lax
from jax.experimental import pallas as pl
from jax.experimental.pallas import tpu as pltpu
from jax.sharding import PartitionSpec as P

EPSILON = 1e-05
NEGATIVE_FILL = -1e30
NEAR = 8
FAR = 4
SHARD = 128
ROW = NEAR * SHARD
CHUNK = 256
CHUNKS = ROW // CHUNK
HEAD = 128
STATE = 256
RIM = 16
DOCS_AT = 4
PAST = 10 * CHUNK
WIDE = 256
STEPS_AT = SHARD
BC_AT = STEPS_AT + RIM
SIDE_AT = BC_AT + 2 * SHARD
SIDE = 16
PACK_ROWS = SIDE_AT + 2 * SIDE
EXP2_SCALE = math.log2(math.e) / math.sqrt(HEAD)
F32 = jnp.float32
BF16 = jnp.bfloat16


def near_groups():
    return [[x * NEAR + z for z in range(NEAR)] for x in range(FAR)]


def far_groups():
    return [[x * NEAR + z for x in range(FAR)] for z in range(NEAR)]


def exchange_near(x):
    return lax.all_to_all(x, "ctx", 0, 0, axis_index_groups=near_groups(), tiled=True)


def from_row_behind(x, by):
    pairs = [(x0 * NEAR + z, (x0 + by) * NEAR + z) for x0 in range(FAR - by) for z in range(NEAR)]
    return lax.ppermute(x, "ctx", pairs)


def from_shard_behind(x):
    return lax.ppermute(x, "ctx", [(i, i + 1) for i in range(NEAR * FAR - 1)])


def with_partner(x):
    count = lax.axis_size("tp")
    return lax.ppermute(x, "tp", [(t, t ^ 1) for t in range(count)])


def first_tokens(info, pos):
    begin = jnp.int32(0)
    first = pos
    for d in range(DOCS_AT, info.shape[0]):
        first = jnp.where(pos >= begin, begin, first)
        begin = begin + info[d]
    return first


def columns_of(rows):
    count = rows[0].shape[1]
    rows = list(rows) + [jnp.zeros((1, count), F32)] * (8 - len(rows))
    return jnp.transpose(jnp.concatenate(rows, 0))


def silu(v):
    return v / (1.0 + jnp.exp(-v))


def pack_kernel(info, queries, steps, raw, rim, taps, side, out, ext):
    ext[0:RIM] = rim[:, NEAR * HEAD :].astype(F32)
    ext[RIM:] = raw[...].astype(F32)
    pos = info[3] + lax.broadcasted_iota(jnp.int32, (1, SHARD), 1)
    since = columns_of([(pos - first_tokens(info, pos)).astype(F32)])[:, 0:1]
    acc = jnp.zeros((SHARD, STATE), F32)
    for m in range(4):
        part = ext[RIM - m : RIM - m + SHARD] * taps[3 - m : 4 - m]
        acc = acc + jnp.where(since >= m, part, 0.0)
    convolved = silu(acc).astype(BF16)
    wide = jnp.concatenate([steps[...], jnp.zeros((SHARD, HEAD - 2 * NEAR), F32)], 1)
    rows = jnp.transpose(wide)
    high = rows.astype(BF16).astype(F32)
    middle = (rows - high).astype(BF16).astype(F32)
    low = rows - high - middle
    for n in range(NEAR):
        out[n, 0:SHARD] = queries[:, n * HEAD : (n + 1) * HEAD]
        two = slice(2 * n, 2 * n + 2)
        behind = rim[:, n * HEAD : (n + 1) * HEAD].astype(F32)
        out[n, STEPS_AT:BC_AT] = jnp.concatenate(
            [high[two], middle[two], low[two], jnp.zeros((2, HEAD), F32), behind[RIM // 2 :]], 0
        ).astype(BF16)
        out[n, BC_AT : BC_AT + SHARD] = convolved[:, 0:HEAD]
        out[n, BC_AT + SHARD : SIDE_AT] = convolved[:, HEAD:]
        out[n, SIDE_AT:] = side[...]


def two_heads(first, second, shape):
    lane = lax.broadcasted_iota(jnp.int32, shape, 1)
    return jnp.where(lane < HEAD // 2, jnp.broadcast_to(first, shape), jnp.broadcast_to(second, shape))


def steps_of(received):
    pieces = []
    for s in range(NEAR):
        piece = received[s, STEPS_AT:BC_AT].astype(F32)
        pieces.append(piece[0:2] + piece[2:4] + piece[4:6])
    return jnp.concatenate(pieces, 1)


def decays_of(steps, rates, near):
    rate = jnp.concatenate(
        [jnp.full((1, ROW), rates[2 * near], F32), jnp.full((1, ROW), rates[2 * near + 1], F32)], 0
    )
    log_decay = -rate * steps
    stacked = jnp.concatenate(
        [log_decay[:, k * CHUNK : (k + 1) * CHUNK] for k in range(CHUNKS)], 0
    )
    high = stacked.astype(BF16)
    rest = stacked - high.astype(F32)
    middle = rest.astype(BF16)
    low = (rest - middle.astype(F32)).astype(BF16)
    below = lax.broadcasted_iota(jnp.int32, (CHUNK, CHUNK), 0)
    across = lax.broadcasted_iota(jnp.int32, (CHUNK, CHUNK), 1)
    upper = jnp.where(below <= across, 1.0, 0.0).astype(BF16)
    summed = jnp.dot(
        jnp.concatenate([high, middle, low, jnp.zeros_like(high)], 0),
        upper,
        preferred_element_type=F32,
    )
    summed = summed[0:8] + (summed[8:16] + summed[16:24])
    locals_ = [summed[2 * k : 2 * k + 2] for k in range(CHUNKS)]
    return locals_, [local[:, CHUNK - 1 : CHUNK] for local in locals_]


def places_kernel(info, seen):
    row_start = info[0]
    pos = row_start + lax.broadcasted_iota(jnp.int32, (1, ROW), 1)
    first = first_tokens(info, pos)
    columns = columns_of([(first - row_start).astype(F32)])
    seen[...] = jnp.broadcast_to(columns[:, 0:1], (ROW, HEAD))


def chunk_weights(steps, local, total, pos, last_start, chunk_start):
    gap = jnp.where(pos >= last_start, total - local, NEGATIVE_FILL)
    crossing = jnp.where(last_start < chunk_start, jnp.exp(total), 0.0)
    return jnp.exp(gap) * steps, jnp.broadcast_to(crossing, (2, STATE))


def weights_kernel(info, rates, received, weigh, decays):
    steps = steps_of(received)
    locals_, totals = decays_of(steps, rates, info[1])
    row_start = info[0]
    pos = row_start + lax.broadcasted_iota(jnp.int32, (1, ROW), 1)
    first = first_tokens(info, pos)
    rows_, decay_rows = [], []
    for k in range(CHUNKS):
        rows = slice(k * CHUNK, (k + 1) * CHUNK)
        last_start = first[:, (k + 1) * CHUNK - 1 : (k + 1) * CHUNK]
        w, decay = chunk_weights(
            steps[:, rows], locals_[k], totals[k], pos[:, rows], last_start, row_start + k * CHUNK
        )
        rows_.append(w)
        decay_rows.append(decay)
    w = jnp.concatenate(rows_, 1)
    columns = columns_of([w[0:1], w[1:2]])
    weigh[...] = two_heads(columns[:, 0:1], columns[:, 1:2], (ROW, HEAD))
    whole = totals[0] + totals[1] + totals[2] + totals[3]
    last = jnp.where(first[:, ROW - 1 : ROW] < row_start, jnp.exp(whole), 0.0)
    decay_rows.append(jnp.broadcast_to(last, (2, STATE)))
    decays[...] = jnp.concatenate(decay_rows + [jnp.zeros((6, STATE), F32)], 0)


def two_head_rows(pair):
    shape = (HEAD, STATE)
    channel = lax.broadcasted_iota(jnp.int32, shape, 0)
    return jnp.where(
        channel < HEAD // 2,
        jnp.broadcast_to(pair[0:1], shape),
        jnp.broadcast_to(pair[1:2], shape),
    )


def dot_rows(left, right):
    return lax.dot_general(left, right, (((1,), (1,)), ((), ())), preferred_element_type=F32)


def chunk_of(choose_mine, received, other, k):
    halves = []
    two = slice(2 * k, 2 * k + 2)
    for half in range(2):
        mine = received[two, BC_AT + half * SHARD : BC_AT + (half + 1) * SHARD]
        theirs = other[two, half * SHARD : (half + 1) * SHARD]
        halves.append(jnp.where(choose_mine, mine, theirs))
    return jnp.concatenate([half.reshape(CHUNK, HEAD) for half in halves], 1)


def masked(raw, offset, seen_rows, diagonal, halved=False):
    count = raw.shape[0]
    slabs = []
    for n in range(raw.shape[1] // HEAD):
        place = lax.broadcasted_iota(jnp.int32, (1, HEAD), 1) + n * HEAD
        if halved:
            rest = jnp.where(place < SHARD + SIDE, place - SIDE, place)
            first = jnp.where(place < SIDE, place, place + (SHARD - SIDE))
            place = jnp.where(place < 2 * SIDE, first, rest)
        place = place + offset
        visible = place.astype(F32) >= seen_rows
        if diagonal is not None:
            down = lax.broadcasted_iota(jnp.int32, (count, HEAD), 0) + diagonal
            along = lax.broadcasted_iota(jnp.int32, (count, HEAD), 1) + n * HEAD
            visible = visible & (along <= down)
        slabs.append(jnp.where(visible, raw[:, n * HEAD : (n + 1) * HEAD], NEGATIVE_FILL))
    return slabs


def largest_of(slabs):
    most = slabs[0]
    for slab in slabs[1:]:
        most = jnp.maximum(most, slab)
    return jnp.max(most, axis=1, keepdims=True)


def weighed(slabs, new_top):
    parts, sums = [], None
    for slab in slabs:
        weight = jnp.exp2((slab - new_top) * EXP2_SCALE)
        sums = weight if sums is None else sums + weight
        parts.append(weight.astype(BF16))
    return sums, parts


def attend_own_kernel(received, own, seen, top, total, summed):
    raws, weights = [], [[] for _ in range(CHUNKS)]
    for j in range(CHUNKS):
        query = received[2 * j :, 0:SHARD, :].reshape(ROW - j * CHUNK, HEAD)
        at = slice(j * CHUNK, (j + 1) * CHUNK)
        raws.append(dot_rows(query, own[at, 0:HEAD]))
    for i in range(CHUNKS):
        rows = slice(i * CHUNK, (i + 1) * CHUNK)
        slabs = []
        for j in range(i + 1):
            raw = raws[j][(i - j) * CHUNK : (i - j + 1) * CHUNK]
            slabs += masked(raw, j * CHUNK, seen[rows], 0 if i == j else None)
        first_top = jnp.broadcast_to(largest_of(slabs), (CHUNK, HEAD))
        sums, parts = weighed(slabs, first_top)
        top[rows] = first_top
        total[rows] = sums
        for j in range(i + 1):
            weights[j].append(jnp.concatenate(parts[2 * j : 2 * j + 2], 1))
    for j in range(CHUNKS):
        values = own[j * CHUNK : (j + 1) * CHUNK, HEAD:]
        product = jnp.dot(jnp.concatenate(weights[j], 0), values, preferred_element_type=F32)
        rows = slice(j * CHUNK, ROW)
        summed[rows] = product if j == 0 else summed[rows] + product


def attend_kernel(
    info,
    received,
    back1,
    back2,
    back3,
    seen,
    top_in,
    total_in,
    summed_in,
    attended,
    top,
    total,
    summed,
    halo_seen,
    halo_top,
    halo_total,
    halo_summed,
):
    row_start = info[0]
    halo_pos = row_start - RIM + lax.broadcasted_iota(jnp.int32, (1, HEAD), 1)
    halo_first = columns_of([(first_tokens(info, halo_pos) - row_start).astype(F32)])
    halo_seen[...] = jnp.broadcast_to(halo_first[0:RIM, 0:1], (RIM, HEAD))
    begin = jnp.int32(0)
    cross_start, cross_end = jnp.int32(0), jnp.int32(0)
    for d in range(DOCS_AT, info.shape[0]):
        inside = begin <= row_start
        cross_start = jnp.where(inside, begin, cross_start)
        begin = begin + info[d]
        cross_end = jnp.where(inside, begin, cross_end)
    reached = cross_end - row_start
    wide_blocks = PAST // WIDE
    lowest = lax.div(cross_start - row_start + PAST, jnp.int32(WIDE))

    def keys_of(back, within):
        at = pl.ds(pl.multiple_of(within * WIDE, WIDE), WIDE)
        return back[at, 0:HEAD], back[at, HEAD:]

    def halved_keys_of(back, within):
        two = pl.ds(2 * within, 2)
        first = received[two, SIDE_AT : SIDE_AT + SIDE, :], received[two, SIDE_AT + SIDE :, :]
        second = back[two, :, 0:HEAD], back[two, :, HEAD:]
        return [
            jnp.concatenate([x.reshape(-1, HEAD), y.reshape(-1, HEAD)], 0)
            for x, y in zip(first, second)
        ]

    def fold(
        query, keys, values, block, seen_ref, top_ref, total_ref, summed_ref, rows, diagonal, halved
    ):
        raw = dot_rows(query, keys)
        slabs = masked(raw, block * WIDE - PAST, seen_ref[rows], diagonal, halved)
        old_top = top_ref[rows]
        new_top = jnp.maximum(old_top, largest_of(slabs))
        factor = jnp.exp2((old_top - new_top) * EXP2_SCALE)
        sums, parts = weighed(slabs, new_top)
        product = jnp.dot(
            jnp.concatenate(parts, 1), values, preferred_element_type=F32
        )
        top_ref[rows] = new_top
        total_ref[rows] = total_ref[rows] * factor + sums
        summed_ref[rows] = summed_ref[rows] * factor + product

    top[...] = top_in[...]
    total[...] = total_in[...]
    summed[...] = summed_in[...]
    halo_top[...] = jnp.full((RIM, HEAD), NEGATIVE_FILL, F32)
    halo_total[...] = jnp.zeros((RIM, HEAD), F32)
    halo_summed[...] = jnp.zeros((RIM, HEAD), F32)

    halo_query = received[0, STEPS_AT:BC_AT]

    def earlier(count):
        query = received[0 : 2 * count, 0:SHARD, :].reshape(count * CHUNK, HEAD)
        for back, begin, blocks in ((back1, 6, 4), (back2, 2, 4), (back3, 0, 2)):
            halved = back is back2

            def visit(n, carry):
                within = blocks - 1 - n
                block = begin + within
                keys, values = (halved_keys_of if halved else keys_of)(back, within)
                fold(
                    query,
                    keys,
                    values,
                    block,
                    seen,
                    top,
                    total,
                    summed,
                    slice(0, count * CHUNK),
                    None,
                    halved,
                )
                fold(
                    halo_query,
                    keys,
                    values,
                    block,
                    halo_seen,
                    halo_top,
                    halo_total,
                    halo_summed,
                    slice(0, RIM),
                    (PAST - RIM) - block * WIDE if back is back1 else None,
                    halved,
                )
                return carry

            lax.fori_loop(0, jnp.clip(begin + blocks - lowest, 0, blocks), visit, 0)

    @pl.when(reached <= CHUNK)
    def _():
        earlier(1)

    @pl.when((reached > CHUNK) & (reached <= 2 * CHUNK))
    def _():
        earlier(2)

    @pl.when(reached > 2 * CHUNK)
    def _():
        earlier(CHUNKS)

    def finish(total_ref, summed_ref):
        whole = jnp.sum(total_ref[...], axis=1, keepdims=True)
        return (summed_ref[...] / jnp.maximum(whole, 0.5)).astype(BF16)

    attended[0:RIM] = finish(halo_total, halo_summed)
    attended[RIM:] = finish(total, summed)


def scan_kernel(
    info, attended, received, other, taps, weigh, decays, seen, x_out, handed, ext
):
    ext[...] = attended[...].astype(F32)
    near = info[1]
    own_taps = taps[:, pl.ds(pl.multiple_of(near * HEAD, HEAD), HEAD)]
    core_zero = info[2] == 0
    state = jnp.zeros((HEAD, STATE), F32)
    for k in range(CHUNKS):
        rows = slice(k * CHUNK, (k + 1) * CHUNK)
        acc = jnp.zeros((CHUNK, HEAD), F32)
        place = lax.broadcasted_iota(jnp.int32, (CHUNK, HEAD), 0) + k * CHUNK
        since = place.astype(F32) - seen[rows]
        for m in range(4):
            part = ext[RIM - m + k * CHUNK : RIM - m + (k + 1) * CHUNK] * own_taps[3 - m : 4 - m]
            acc = acc + jnp.where(since >= m, part, 0.0)
        x = silu(acc).astype(BF16)
        x_out[rows] = x
        weighed = (x.astype(F32) * weigh[rows]).astype(BF16)
        added = lax.dot_general(
            weighed,
            chunk_of(core_zero, received, other, k),
            (((0,), (0,)), ((), ())),
            preferred_element_type=F32,
        )
        state = state * two_head_rows(decays[2 * k : 2 * k + 2]) + added
    decay = decays[2 * CHUNKS : 2 * CHUNKS + 2]
    high = decay.astype(BF16).astype(F32)
    tail = jnp.concatenate([high, decay - high, jnp.zeros((12, STATE), F32)], 0).astype(BF16)
    state = state.astype(BF16)
    for r in range(FAR):
        handed[r, 0:HEAD] = state
        handed[r, HEAD:] = tail


def inner_kernel(
    info, rates, received, other, x_in, y_out, enter_row, c_out
):
    near = info[1]
    core_zero = info[2] == 0
    steps = steps_of(received)
    locals_, totals = decays_of(steps, rates, near)
    row_start = info[0]
    pos = row_start + lax.broadcasted_iota(jnp.int32, (1, ROW), 1)
    first = first_tokens(info, pos)
    below = lax.broadcasted_iota(jnp.int32, (CHUNK, CHUNK), 0)
    across = lax.broadcasted_iota(jnp.int32, (CHUNK, CHUNK), 1)
    causal = across <= below
    place = across.astype(F32)
    gains_at = 2 * NEAR + 2 * near
    gain = two_heads(rates[gains_at], rates[gains_at + 1], (1, HEAD))
    shape = (CHUNK, HEAD)
    before = jnp.zeros((2, 1), F32)
    for k in range(CHUNKS):
        rows = slice(k * CHUNK, (k + 1) * CHUNK)
        chunk_start = row_start + k * CHUNK
        local = locals_[k]
        e_chunk = jnp.exp(jnp.where(first[:, rows] < chunk_start, local, NEGATIVE_FILL))
        e_row = jnp.exp(jnp.where(first[:, rows] < row_start, before + local, NEGATIVE_FILL))
        before = before + totals[k]
        last_start = first[:, (k + 1) * CHUNK - 1 : (k + 1) * CHUNK]
        w, decay = chunk_weights(
            steps[:, rows], local, totals[k], pos[:, rows], last_start, chunk_start
        )
        columns = jnp.transpose(jnp.concatenate([e_chunk, e_row, local, w], 0))
        since = columns_of([(first[:, rows] - chunk_start).astype(F32)])[:, 0:1]
        enter_row[rows] = two_heads(columns[:, 2:3], columns[:, 3:4], shape)
        c_values = chunk_of(jnp.logical_not(core_zero), received, other, k)
        c_out[rows] = c_values
        b_values = chunk_of(core_zero, received, other, k)
        gram = dot_rows(c_values, b_values)
        visible = causal & (place >= since)
        x = x_in[rows]
        halves = []
        for h in range(2):
            gap = jnp.where(visible, columns[:, 4 + h : 5 + h] - local[h : h + 1], NEGATIVE_FILL)
            mix = (gram * jnp.exp(gap) * steps[h : h + 1, rows]).astype(BF16)
            halves.append(jnp.dot(mix, x, preferred_element_type=F32))
        lane = lax.broadcasted_iota(jnp.int32, shape, 1)
        y = jnp.where(lane < HEAD // 2, halves[0], halves[1]) + x.astype(F32) * gain
        if k > 0:
            carried = dot_rows(c_values, state.astype(BF16))
            y = y + two_heads(columns[:, 0:1], columns[:, 1:2], shape) * carried
        y_out[rows] = y
        if k + 1 < CHUNKS:
            weighed = x.astype(F32) * two_heads(columns[:, 6:7], columns[:, 7:8], shape)
            added = lax.dot_general(
                weighed.astype(BF16),
                b_values,
                (((0,), (0,)), ((), ())),
                preferred_element_type=F32,
            )
            state = added if k == 0 else state * two_head_rows(decay) + added


def carried_kernel(info, y_in, enter_row, c_in, handed, y_out):
    entering = jnp.zeros((HEAD, STATE), F32)
    for r in range(FAR - 1):
        tail = handed[r, HEAD:].astype(F32)
        decay = two_head_rows(tail[0:2] + tail[2:4])
        following = entering * decay + handed[r, 0:HEAD].astype(F32)
        entering = jnp.where(r * ROW < info[0], following, entering)
    entering = entering.astype(BF16)
    for k in range(CHUNKS):
        rows = slice(k * CHUNK, (k + 1) * CHUNK)
        carried = dot_rows(c_in[rows], entering)
        y_out[rows] = (y_in[rows] + enter_row[rows] * carried).astype(BF16)


def gated_of(y, gate, h):
    return y[h].astype(F32) * silu(gate[:, h * HEAD : (h + 1) * HEAD].astype(F32))


def square_kernel(y, gate, sums):
    acc = jnp.zeros((SHARD, HEAD), F32)
    for h in range(NEAR):
        gated = gated_of(y, gate, h)
        acc = acc + gated * gated
    sums[...] = jnp.broadcast_to(jnp.sum(acc, axis=1, keepdims=True), (SHARD, HEAD))


def norm_kernel(y, gate, sums, partner, gain, out):
    mean = (sums[...] + partner[...]) / (2.0 * NEAR * HEAD)
    scale = lax.rsqrt(mean + EPSILON)
    for h in range(NEAR):
        columns = slice(h * HEAD, (h + 1) * HEAD)
        out[:, columns] = (gated_of(y, gate, h) * scale * gain[:, columns]).astype(BF16)


def call(kernel, outs, args, smem=0, raw=(), raw_out=False, scratch=(), flops=0, mib=4):
    specs = []
    for n in range(len(args)):
        if n < smem:
            specs.append(pl.BlockSpec(memory_space=pltpu.SMEM))
        elif n in raw:
            specs.append(pl.BlockSpec(memory_space=pl.ANY))
        else:
            specs.append(pl.BlockSpec(memory_space=pltpu.VMEM))
    single = len(outs) == 1
    shapes = [jax.ShapeDtypeStruct(shape, kind) for shape, kind in outs]
    out_specs = [pl.BlockSpec(memory_space=pl.ANY if raw_out else pltpu.VMEM)] * len(outs)
    return pl.pallas_call(
        kernel,
        out_shape=shapes[0] if single else shapes,
        in_specs=specs,
        out_specs=out_specs[0] if single else out_specs,
        scratch_shapes=list(scratch),
        compiler_params=pltpu.CompilerParams(vmem_limit_bytes=mib * 1024 * 1024),
        cost_estimate=pl.CostEstimate(flops=flops, bytes_accessed=1 << 21, transcendentals=0),
    )(*args)


def run_attend(info, received, *args):
    return call(
        attend_kernel,
        [((RIM + ROW, HEAD), BF16)],
        (info, received, *args),
        smem=1,
        scratch=[
            pltpu.VMEM((ROW, HEAD), F32),
            pltpu.VMEM((ROW, HEAD), F32),
            pltpu.VMEM((ROW, HEAD), F32),
            pltpu.VMEM((RIM, HEAD), F32),
            pltpu.VMEM((RIM, HEAD), F32),
            pltpu.VMEM((RIM, HEAD), F32),
            pltpu.VMEM((RIM, HEAD), F32),
        ],
        flops=1 << 32,
        mib=7,
    )


def run_scan(info, attended, received, other, taps, weigh, decays, seen):
    return call(
        scan_kernel,
        [
            ((ROW, HEAD), BF16),
            ((FAR, HEAD + 16, STATE), BF16),
        ],
        (info, attended, received, other, taps, weigh, decays, seen),
        smem=1,
        scratch=[pltpu.VMEM((RIM + ROW, HEAD), F32)],
    )


def on_device(
    queries,
    key_rows,
    value_rows,
    doc_lengths,
    gate_input,
    bc_input,
    step_size,
    decay_rate,
    skip_gain,
    conv_x,
    conv_bc,
    norm_gain,
):
    ctx = lax.axis_index("ctx")
    tp = lax.axis_index("tp")
    near = ctx % NEAR
    core = tp % 2
    group = tp // 2
    place = jnp.stack([(ctx // NEAR) * ROW, near, core, ctx * SHARD]).astype(jnp.int32)
    info = jnp.concatenate([place, doc_lengths])
    rates = jnp.concatenate([decay_rate, skip_gain])

    bc_mine = lax.dynamic_slice(bc_input, (0, core, group, 0), (SHARD, 1, 1, STATE)).reshape(
        SHARD, STATE
    )
    taps_mine = lax.dynamic_slice(conv_bc, (0, core, group, 0), (4, 1, 1, STATE)).reshape(4, STATE)
    rim = from_shard_behind(jnp.concatenate([queries[SHARD - RIM :], bc_mine[SHARD - RIM :]], 1))
    wide = (NEAR, SHARD, 2 * HEAD)
    pairs = jnp.where(
        lax.broadcasted_iota(jnp.int32, wide, 2) < HEAD,
        jnp.broadcast_to(jnp.pad(key_rows, ((0, 0), (0, HEAD))), wide),
        jnp.broadcast_to(jnp.pad(value_rows, ((0, 0), (HEAD, 0))), wide),
    )
    side = from_row_behind(jnp.concatenate([key_rows[:SIDE], value_rows[:SIDE]], 0), 2)
    own = exchange_near(pairs.reshape(ROW, 2 * HEAD))
    seen = call(places_kernel, [((ROW, HEAD), F32)], (info,), smem=1)
    packed = call(
        pack_kernel,
        [((NEAR, PACK_ROWS, HEAD), BF16)],
        (info, queries, step_size, bc_mine, rim, taps_mine, side),
        smem=1,
        scratch=[pltpu.VMEM((RIM + SHARD, STATE), F32)],
    )
    own, packed = lax.optimization_barrier((own, packed))
    half = ROW // 2
    back1 = from_row_behind(own, 1)
    back2 = from_row_behind(own.reshape(NEAR, SHARD, 2 * HEAD)[:, SIDE:], 2)
    back3 = from_row_behind(own[half:], 3)
    received = exchange_near(packed.reshape(NEAR * PACK_ROWS, HEAD)).reshape(
        NEAR, PACK_ROWS, HEAD
    )
    weigh, decays = call(
        weights_kernel,
        [((ROW, HEAD), F32), ((16, STATE), F32)],
        (info, rates, received),
        smem=2,
    )
    own_part = call(attend_own_kernel, [((ROW, HEAD), F32)] * 3, (received, own, seen), mib=7)
    received, weigh, back1, back2, back3, *own_part = lax.optimization_barrier(
        (received, weigh, back1, back2, back3, *own_part)
    )
    other = with_partner(received[:, BC_AT:SIDE_AT])
    attended = run_attend(info, received, back1, back2, back3, seen, *own_part)
    x, handed = run_scan(info, attended, received, other, conv_x, weigh, decays, seen)
    handed = lax.all_to_all(
        handed.reshape(FAR * (HEAD + 16), STATE),
        "ctx",
        0,
        0,
        axis_index_groups=far_groups(),
        tiled=True,
    ).reshape(FAR, HEAD + 16, STATE)
    y_inner, enter_row, c_row = call(
        inner_kernel,
        [((ROW, HEAD), F32), ((ROW, HEAD), F32), ((ROW, STATE), BF16)],
        (info, rates, received, other, x),
        smem=2,
        flops=1 << 30,
    )
    y_row = call(
        carried_kernel,
        [((ROW, HEAD), BF16)],
        (info, y_inner, enter_row, c_row, handed),
        smem=1,
    )
    y_heads = exchange_near(y_row).reshape(NEAR, SHARD, HEAD)
    sums = call(square_kernel, [((SHARD, HEAD), F32)], (y_heads, gate_input))
    partner = with_partner(sums)
    return call(
        norm_kernel,
        [((SHARD, NEAR * HEAD), BF16)],
        (y_heads, gate_input, sums, partner, norm_gain.reshape(1, -1)),
    )


def solution(mesh):
    return jax.shard_map(
        on_device,
        mesh=mesh,
        in_specs=(
            P("ctx", "tp"),
            P("ctx", "tp"),
            P("ctx", "tp"),
            P(),
            P("ctx", "tp"),
            P("ctx", None, None, None),
            P("ctx", "tp"),
            P("tp"),
            P("tp"),
            P(None, "tp"),
            P(),
            P("tp"),
        ),
        out_specs=P("ctx", "tp"),
        check_vma=False,
    )
```

```python
import math

import jax
import jax.numpy as jnp
from jax import lax
from jax.experimental import pallas as pl
from jax.experimental.pallas import tpu as pltpu
from jax.sharding import PartitionSpec as P

EPSILON = 1e-05
NEGATIVE_FILL = -1e30
NEAR = 8
FAR = 4
SHARD = 128
ROW = NEAR * SHARD
CHUNK = 256
CHUNKS = ROW // CHUNK
HEAD = 128
STATE = 256
RIM = 16
DOCS_AT = 4
PAST = 10 * CHUNK
WIDE = 256
STEPS_AT = SHARD
BC_AT = STEPS_AT + RIM
SIDE_AT = BC_AT + 2 * SHARD
SIDE = 16
PACK_ROWS = SIDE_AT + 2 * SIDE
EXP2_SCALE = math.log2(math.e) / math.sqrt(HEAD)
F32 = jnp.float32
BF16 = jnp.bfloat16


def near_groups():
    return [[x * NEAR + z for z in range(NEAR)] for x in range(FAR)]


def far_groups():
    return [[x * NEAR + z for x in range(FAR)] for z in range(NEAR)]


def exchange_near(x):
    return lax.all_to_all(x, "ctx", 0, 0, axis_index_groups=near_groups(), tiled=True)


def from_row_behind(x, by):
    pairs = [(x0 * NEAR + z, (x0 + by) * NEAR + z) for x0 in range(FAR - by) for z in range(NEAR)]
    return lax.ppermute(x, "ctx", pairs)


def from_shard_behind(x):
    return lax.ppermute(x, "ctx", [(i, i + 1) for i in range(NEAR * FAR - 1)])


def with_partner(x):
    count = lax.axis_size("tp")
    return lax.ppermute(x, "tp", [(t, t ^ 1) for t in range(count)])


def first_tokens(info, pos):
    begin = jnp.int32(0)
    first = pos
    for d in range(DOCS_AT, info.shape[0]):
        first = jnp.where(pos >= begin, begin, first)
        begin = begin + info[d]
    return first


def columns_of(rows):
    count = rows[0].shape[1]
    rows = list(rows) + [jnp.zeros((1, count), F32)] * (8 - len(rows))
    return jnp.transpose(jnp.concatenate(rows, 0))


def silu(v):
    return v / (1.0 + jnp.exp(-v))


def pack_kernel(info, queries, steps, raw, rim, taps, side, out, ext):
    ext[0:RIM] = rim[:, NEAR * HEAD :].astype(F32)
    ext[RIM:] = raw[...].astype(F32)
    pos = info[3] + lax.broadcasted_iota(jnp.int32, (1, SHARD), 1)
    since = columns_of([(pos - first_tokens(info, pos)).astype(F32)])[:, 0:1]
    acc = jnp.zeros((SHARD, STATE), F32)
    for m in range(4):
        part = ext[RIM - m : RIM - m + SHARD] * taps[3 - m : 4 - m]
        acc = acc + jnp.where(since >= m, part, 0.0)
    convolved = silu(acc).astype(BF16)
    wide = jnp.concatenate([steps[...], jnp.zeros((SHARD, HEAD - 2 * NEAR), F32)], 1)
    rows = jnp.transpose(wide)
    high = rows.astype(BF16).astype(F32)
    middle = (rows - high).astype(BF16).astype(F32)
    low = rows - high - middle
    for n in range(NEAR):
        out[n, 0:SHARD] = queries[:, n * HEAD : (n + 1) * HEAD]
        two = slice(2 * n, 2 * n + 2)
        behind = rim[:, n * HEAD : (n + 1) * HEAD].astype(F32)
        out[n, STEPS_AT:BC_AT] = jnp.concatenate(
            [high[two], middle[two], low[two], jnp.zeros((2, HEAD), F32), behind[RIM // 2 :]], 0
        ).astype(BF16)
        out[n, BC_AT : BC_AT + SHARD] = convolved[:, 0:HEAD]
        out[n, BC_AT + SHARD : SIDE_AT] = convolved[:, HEAD:]
        out[n, SIDE_AT:] = side[...]


def two_heads(first, second, shape):
    lane = lax.broadcasted_iota(jnp.int32, shape, 1)
    return jnp.where(lane < HEAD // 2, jnp.broadcast_to(first, shape), jnp.broadcast_to(second, shape))


def steps_of(received):
    pieces = []
    for s in range(NEAR):
        piece = received[s, STEPS_AT:BC_AT].astype(F32)
        pieces.append(piece[0:2] + piece[2:4] + piece[4:6])
    return jnp.concatenate(pieces, 1)


def decays_of(steps, rates, near):
    rate = jnp.concatenate(
        [jnp.full((1, ROW), rates[2 * near], F32), jnp.full((1, ROW), rates[2 * near + 1], F32)], 0
    )
    log_decay = -rate * steps
    stacked = jnp.concatenate(
        [log_decay[:, k * CHUNK : (k + 1) * CHUNK] for k in range(CHUNKS)], 0
    )
    high = stacked.astype(BF16)
    rest = stacked - high.astype(F32)
    middle = rest.astype(BF16)
    low = (rest - middle.astype(F32)).astype(BF16)
    below = lax.broadcasted_iota(jnp.int32, (CHUNK, CHUNK), 0)
    across = lax.broadcasted_iota(jnp.int32, (CHUNK, CHUNK), 1)
    upper = jnp.where(below <= across, 1.0, 0.0).astype(BF16)
    summed = jnp.dot(
        jnp.concatenate([high, middle, low, jnp.zeros_like(high)], 0),
        upper,
        preferred_element_type=F32,
    )
    summed = summed[0:8] + (summed[8:16] + summed[16:24])
    locals_ = [summed[2 * k : 2 * k + 2] for k in range(CHUNKS)]
    return locals_, [local[:, CHUNK - 1 : CHUNK] for local in locals_]


def places_kernel(info, seen):
    row_start = info[0]
    pos = row_start + lax.broadcasted_iota(jnp.int32, (1, ROW), 1)
    first = first_tokens(info, pos)
    columns = columns_of([(first - row_start).astype(F32)])
    seen[...] = jnp.broadcast_to(columns[:, 0:1], (ROW, HEAD))


def chunk_weights(steps, local, total, pos, last_start, chunk_start):
    gap = jnp.where(pos >= last_start, total - local, NEGATIVE_FILL)
    crossing = jnp.where(last_start < chunk_start, jnp.exp(total), 0.0)
    return jnp.exp(gap) * steps, jnp.broadcast_to(crossing, (2, STATE))


def weights_kernel(info, rates, received, weigh, decays):
    steps = steps_of(received)
    locals_, totals = decays_of(steps, rates, info[1])
    row_start = info[0]
    pos = row_start + lax.broadcasted_iota(jnp.int32, (1, ROW), 1)
    first = first_tokens(info, pos)
    rows_, decay_rows = [], []
    for k in range(CHUNKS):
        rows = slice(k * CHUNK, (k + 1) * CHUNK)
        last_start = first[:, (k + 1) * CHUNK - 1 : (k + 1) * CHUNK]
        w, decay = chunk_weights(
            steps[:, rows], locals_[k], totals[k], pos[:, rows], last_start, row_start + k * CHUNK
        )
        rows_.append(w)
        decay_rows.append(decay)
    w = jnp.concatenate(rows_, 1)
    columns = columns_of([w[0:1], w[1:2]])
    weigh[...] = two_heads(columns[:, 0:1], columns[:, 1:2], (ROW, HEAD))
    whole = totals[0] + totals[1] + totals[2] + totals[3]
    last = jnp.where(first[:, ROW - 1 : ROW] < row_start, jnp.exp(whole), 0.0)
    decay_rows.append(jnp.broadcast_to(last, (2, STATE)))
    decays[...] = jnp.concatenate(decay_rows + [jnp.zeros((6, STATE), F32)], 0)


def two_head_rows(pair):
    shape = (HEAD, STATE)
    channel = lax.broadcasted_iota(jnp.int32, shape, 0)
    return jnp.where(
        channel < HEAD // 2,
        jnp.broadcast_to(pair[0:1], shape),
        jnp.broadcast_to(pair[1:2], shape),
    )


def dot_rows(left, right):
    return lax.dot_general(left, right, (((1,), (1,)), ((), ())), preferred_element_type=F32)


def chunk_of(choose_mine, received, other, k):
    halves = []
    two = slice(2 * k, 2 * k + 2)
    for half in range(2):
        mine = received[two, BC_AT + half * SHARD : BC_AT + (half + 1) * SHARD]
        theirs = other[two, half * SHARD : (half + 1) * SHARD]
        halves.append(jnp.where(choose_mine, mine, theirs))
    return jnp.concatenate([half.reshape(CHUNK, HEAD) for half in halves], 1)


def masked(raw, offset, seen_rows, diagonal, halved=False):
    count = raw.shape[0]
    slabs = []
    for n in range(raw.shape[1] // HEAD):
        place = lax.broadcasted_iota(jnp.int32, (1, HEAD), 1) + n * HEAD
        if halved:
            rest = jnp.where(place < SHARD + SIDE, place - SIDE, place)
            first = jnp.where(place < SIDE, place, place + (SHARD - SIDE))
            place = jnp.where(place < 2 * SIDE, first, rest)
        place = place + offset
        visible = place.astype(F32) >= seen_rows
        if diagonal is not None:
            down = lax.broadcasted_iota(jnp.int32, (count, HEAD), 0) + diagonal
            along = lax.broadcasted_iota(jnp.int32, (count, HEAD), 1) + n * HEAD
            visible = visible & (along <= down)
        slabs.append(jnp.where(visible, raw[:, n * HEAD : (n + 1) * HEAD], NEGATIVE_FILL))
    return slabs


def largest_of(slabs):
    most = slabs[0]
    for slab in slabs[1:]:
        most = jnp.maximum(most, slab)
    return jnp.max(most, axis=1, keepdims=True)


def weighed(slabs, new_top):
    parts, sums = [], None
    for slab in slabs:
        weight = jnp.exp2((slab - new_top) * EXP2_SCALE)
        sums = weight if sums is None else sums + weight
        parts.append(weight.astype(BF16))
    return sums, parts


def attend_own_kernel(received, own, seen, top, total, summed):
    raws, weights = [], [[] for _ in range(CHUNKS)]
    for j in range(CHUNKS):
        query = received[2 * j :, 0:SHARD, :].reshape(ROW - j * CHUNK, HEAD)
        at = slice(j * CHUNK, (j + 1) * CHUNK)
        raws.append(dot_rows(query, own[at, 0:HEAD]))
    for i in range(CHUNKS):
        rows = slice(i * CHUNK, (i + 1) * CHUNK)
        slabs = []
        for j in range(i + 1):
            raw = raws[j][(i - j) * CHUNK : (i - j + 1) * CHUNK]
            slabs += masked(raw, j * CHUNK, seen[rows], 0 if i == j else None)
        first_top = jnp.broadcast_to(largest_of(slabs), (CHUNK, HEAD))
        sums, parts = weighed(slabs, first_top)
        top[rows] = first_top
        total[rows] = sums
        for j in range(i + 1):
            weights[j].append(jnp.concatenate(parts[2 * j : 2 * j + 2], 1))
    for j in range(CHUNKS):
        values = own[j * CHUNK : (j + 1) * CHUNK, HEAD:]
        product = jnp.dot(jnp.concatenate(weights[j], 0), values, preferred_element_type=F32)
        rows = slice(j * CHUNK, ROW)
        summed[rows] = product if j == 0 else summed[rows] + product


def ahead_kernel(info, rates, received, own, seen, weigh, decays, top, total, summed):
    weights_kernel(info, rates, received, weigh, decays)
    attend_own_kernel(received, own, seen, top, total, summed)


def attend_kernel(
    info,
    received,
    back1,
    back2,
    back3,
    seen,
    top_in,
    total_in,
    summed_in,
    attended,
    top,
    total,
    summed,
    halo_seen,
    halo_top,
    halo_total,
    halo_summed,
):
    row_start = info[0]
    halo_pos = row_start - RIM + lax.broadcasted_iota(jnp.int32, (1, HEAD), 1)
    halo_first = columns_of([(first_tokens(info, halo_pos) - row_start).astype(F32)])
    halo_seen[...] = jnp.broadcast_to(halo_first[0:RIM, 0:1], (RIM, HEAD))
    begin = jnp.int32(0)
    cross_start, cross_end = jnp.int32(0), jnp.int32(0)
    for d in range(DOCS_AT, info.shape[0]):
        inside = begin <= row_start
        cross_start = jnp.where(inside, begin, cross_start)
        begin = begin + info[d]
        cross_end = jnp.where(inside, begin, cross_end)
    reached = cross_end - row_start
    wide_blocks = PAST // WIDE
    lowest = lax.div(cross_start - row_start + PAST, jnp.int32(WIDE))

    def keys_of(back, within):
        at = pl.ds(pl.multiple_of(within * WIDE, WIDE), WIDE)
        return back[at, 0:HEAD], back[at, HEAD:]

    def halved_keys_of(back, within):
        two = pl.ds(2 * within, 2)
        first = received[two, SIDE_AT : SIDE_AT + SIDE, :], received[two, SIDE_AT + SIDE :, :]
        second = back[two, :, 0:HEAD], back[two, :, HEAD:]
        return [
            jnp.concatenate([x.reshape(-1, HEAD), y.reshape(-1, HEAD)], 0)
            for x, y in zip(first, second)
        ]

    def fold(
        query, keys, values, block, seen_ref, top_ref, total_ref, summed_ref, rows, diagonal, halved
    ):
        raw = dot_rows(query, keys)
        slabs = masked(raw, block * WIDE - PAST, seen_ref[rows], diagonal, halved)
        old_top = top_ref[rows]
        new_top = jnp.maximum(old_top, largest_of(slabs))
        factor = jnp.exp2((old_top - new_top) * EXP2_SCALE)
        sums, parts = weighed(slabs, new_top)
        product = jnp.dot(
            jnp.concatenate(parts, 1), values, preferred_element_type=F32
        )
        top_ref[rows] = new_top
        total_ref[rows] = total_ref[rows] * factor + sums
        summed_ref[rows] = summed_ref[rows] * factor + product

    top[...] = top_in[...]
    total[...] = total_in[...]
    summed[...] = summed_in[...]
    halo_top[...] = jnp.full((RIM, HEAD), NEGATIVE_FILL, F32)
    halo_total[...] = jnp.zeros((RIM, HEAD), F32)
    halo_summed[...] = jnp.zeros((RIM, HEAD), F32)

    halo_query = received[0, STEPS_AT:BC_AT]

    def earlier(count):
        query = received[0 : 2 * count, 0:SHARD, :].reshape(count * CHUNK, HEAD)
        for back, begin, blocks in ((back1, 6, 4), (back2, 2, 4), (back3, 0, 2)):
            halved = back is back2

            def visit(n, carry):
                within = blocks - 1 - n
                block = begin + within
                keys, values = (halved_keys_of if halved else keys_of)(back, within)
                fold(
                    query,
                    keys,
                    values,
                    block,
                    seen,
                    top,
                    total,
                    summed,
                    slice(0, count * CHUNK),
                    None,
                    halved,
                )
                fold(
                    halo_query,
                    keys,
                    values,
                    block,
                    halo_seen,
                    halo_top,
                    halo_total,
                    halo_summed,
                    slice(0, RIM),
                    (PAST - RIM) - block * WIDE if back is back1 else None,
                    halved,
                )
                return carry

            lax.fori_loop(0, jnp.clip(begin + blocks - lowest, 0, blocks), visit, 0)

    @pl.when(reached <= CHUNK)
    def _():
        earlier(1)

    @pl.when((reached > CHUNK) & (reached <= 2 * CHUNK))
    def _():
        earlier(2)

    @pl.when(reached > 2 * CHUNK)
    def _():
        earlier(CHUNKS)

    def finish(total_ref, summed_ref):
        whole = jnp.sum(total_ref[...], axis=1, keepdims=True)
        return (summed_ref[...] / jnp.maximum(whole, 0.5)).astype(BF16)

    attended[0:RIM] = finish(halo_total, halo_summed)
    attended[RIM:] = finish(total, summed)


def scan_kernel(
    info, attended, received, other, taps, weigh, decays, seen, x_out, handed, ext
):
    ext[...] = attended[...].astype(F32)
    near = info[1]
    own_taps = taps[:, pl.ds(pl.multiple_of(near * HEAD, HEAD), HEAD)]
    core_zero = info[2] == 0
    state = jnp.zeros((HEAD, STATE), F32)
    for k in range(CHUNKS):
        rows = slice(k * CHUNK, (k + 1) * CHUNK)
        acc = jnp.zeros((CHUNK, HEAD), F32)
        place = lax.broadcasted_iota(jnp.int32, (CHUNK, HEAD), 0) + k * CHUNK
        since = place.astype(F32) - seen[rows]
        for m in range(4):
            part = ext[RIM - m + k * CHUNK : RIM - m + (k + 1) * CHUNK] * own_taps[3 - m : 4 - m]
            acc = acc + jnp.where(since >= m, part, 0.0)
        x = silu(acc).astype(BF16)
        x_out[rows] = x
        weighed = (x.astype(F32) * weigh[rows]).astype(BF16)
        added = lax.dot_general(
            weighed,
            chunk_of(core_zero, received, other, k),
            (((0,), (0,)), ((), ())),
            preferred_element_type=F32,
        )
        state = state * two_head_rows(decays[2 * k : 2 * k + 2]) + added
    decay = decays[2 * CHUNKS : 2 * CHUNKS + 2]
    high = decay.astype(BF16).astype(F32)
    tail = jnp.concatenate([high, decay - high, jnp.zeros((12, STATE), F32)], 0).astype(BF16)
    state = state.astype(BF16)
    for r in range(FAR):
        handed[r, 0:HEAD] = state
        handed[r, HEAD:] = tail


def inner_kernel(
    info, rates, received, other, x_in, y_out, enter_row, c_out
):
    near = info[1]
    core_zero = info[2] == 0
    steps = steps_of(received)
    locals_, totals = decays_of(steps, rates, near)
    row_start = info[0]
    pos = row_start + lax.broadcasted_iota(jnp.int32, (1, ROW), 1)
    first = first_tokens(info, pos)
    below = lax.broadcasted_iota(jnp.int32, (CHUNK, CHUNK), 0)
    across = lax.broadcasted_iota(jnp.int32, (CHUNK, CHUNK), 1)
    causal = across <= below
    place = across.astype(F32)
    gains_at = 2 * NEAR + 2 * near
    gain = two_heads(rates[gains_at], rates[gains_at + 1], (1, HEAD))
    shape = (CHUNK, HEAD)
    before = jnp.zeros((2, 1), F32)
    for k in range(CHUNKS):
        rows = slice(k * CHUNK, (k + 1) * CHUNK)
        chunk_start = row_start + k * CHUNK
        local = locals_[k]
        e_chunk = jnp.exp(jnp.where(first[:, rows] < chunk_start, local, NEGATIVE_FILL))
        e_row = jnp.exp(jnp.where(first[:, rows] < row_start, before + local, NEGATIVE_FILL))
        before = before + totals[k]
        last_start = first[:, (k + 1) * CHUNK - 1 : (k + 1) * CHUNK]
        w, decay = chunk_weights(
            steps[:, rows], local, totals[k], pos[:, rows], last_start, chunk_start
        )
        columns = jnp.transpose(jnp.concatenate([e_chunk, e_row, local, w], 0))
        since = columns_of([(first[:, rows] - chunk_start).astype(F32)])[:, 0:1]
        enter_row[rows] = two_heads(columns[:, 2:3], columns[:, 3:4], shape)
        c_values = chunk_of(jnp.logical_not(core_zero), received, other, k)
        c_out[rows] = c_values
        b_values = chunk_of(core_zero, received, other, k)
        gram = dot_rows(c_values, b_values)
        visible = causal & (place >= since)
        x = x_in[rows]
        halves = []
        for h in range(2):
            gap = jnp.where(visible, columns[:, 4 + h : 5 + h] - local[h : h + 1], NEGATIVE_FILL)
            mix = (gram * jnp.exp(gap) * steps[h : h + 1, rows]).astype(BF16)
            halves.append(jnp.dot(mix, x, preferred_element_type=F32))
        lane = lax.broadcasted_iota(jnp.int32, shape, 1)
        y = jnp.where(lane < HEAD // 2, halves[0], halves[1]) + x.astype(F32) * gain
        if k > 0:
            carried = dot_rows(c_values, state.astype(BF16))
            y = y + two_heads(columns[:, 0:1], columns[:, 1:2], shape) * carried
        y_out[rows] = y
        if k + 1 < CHUNKS:
            weighed = x.astype(F32) * two_heads(columns[:, 6:7], columns[:, 7:8], shape)
            added = lax.dot_general(
                weighed.astype(BF16),
                b_values,
                (((0,), (0,)), ((), ())),
                preferred_element_type=F32,
            )
            state = added if k == 0 else state * two_head_rows(decay) + added


def carried_kernel(info, y_in, enter_row, c_in, handed, y_out):
    entering = jnp.zeros((HEAD, STATE), F32)
    for r in range(FAR - 1):
        tail = handed[r, HEAD:].astype(F32)
        decay = two_head_rows(tail[0:2] + tail[2:4])
        following = entering * decay + handed[r, 0:HEAD].astype(F32)
        entering = jnp.where(r * ROW < info[0], following, entering)
    entering = entering.astype(BF16)
    for k in range(CHUNKS):
        rows = slice(k * CHUNK, (k + 1) * CHUNK)
        carried = dot_rows(c_in[rows], entering)
        y_out[rows] = (y_in[rows] + enter_row[rows] * carried).astype(BF16)


def gated_of(y, gate, h):
    return y[h].astype(F32) * silu(gate[:, h * HEAD : (h + 1) * HEAD].astype(F32))


def square_kernel(y, gate, sums):
    acc = jnp.zeros((SHARD, HEAD), F32)
    for h in range(NEAR):
        gated = gated_of(y, gate, h)
        acc = acc + gated * gated
    sums[...] = jnp.broadcast_to(jnp.sum(acc, axis=1, keepdims=True), (SHARD, HEAD))


def norm_kernel(y, gate, sums, partner, gain, out):
    mean = (sums[...] + partner[...]) / (2.0 * NEAR * HEAD)
    scale = lax.rsqrt(mean + EPSILON)
    for h in range(NEAR):
        columns = slice(h * HEAD, (h + 1) * HEAD)
        out[:, columns] = (gated_of(y, gate, h) * scale * gain[:, columns]).astype(BF16)


def call(kernel, outs, args, smem=0, raw=(), raw_out=False, scratch=(), flops=0, mib=4):
    specs = []
    for n in range(len(args)):
        if n < smem:
            specs.append(pl.BlockSpec(memory_space=pltpu.SMEM))
        elif n in raw:
            specs.append(pl.BlockSpec(memory_space=pl.ANY))
        else:
            specs.append(pl.BlockSpec(memory_space=pltpu.VMEM))
    single = len(outs) == 1
    shapes = [jax.ShapeDtypeStruct(shape, kind) for shape, kind in outs]
    out_specs = [pl.BlockSpec(memory_space=pl.ANY if raw_out else pltpu.VMEM)] * len(outs)
    return pl.pallas_call(
        kernel,
        out_shape=shapes[0] if single else shapes,
        in_specs=specs,
        out_specs=out_specs[0] if single else out_specs,
        scratch_shapes=list(scratch),
        compiler_params=pltpu.CompilerParams(vmem_limit_bytes=mib * 1024 * 1024),
        cost_estimate=pl.CostEstimate(flops=flops, bytes_accessed=1 << 21, transcendentals=0),
    )(*args)


def run_attend(info, received, *args):
    return call(
        attend_kernel,
        [((RIM + ROW, HEAD), BF16)],
        (info, received, *args),
        smem=1,
        scratch=[
            pltpu.VMEM((ROW, HEAD), F32),
            pltpu.VMEM((ROW, HEAD), F32),
            pltpu.VMEM((ROW, HEAD), F32),
            pltpu.VMEM((RIM, HEAD), F32),
            pltpu.VMEM((RIM, HEAD), F32),
            pltpu.VMEM((RIM, HEAD), F32),
            pltpu.VMEM((RIM, HEAD), F32),
        ],
        flops=1 << 32,
        mib=7,
    )


def run_scan(info, attended, received, other, taps, weigh, decays, seen):
    return call(
        scan_kernel,
        [
            ((ROW, HEAD), BF16),
            ((FAR, HEAD + 16, STATE), BF16),
        ],
        (info, attended, received, other, taps, weigh, decays, seen),
        smem=1,
        scratch=[pltpu.VMEM((RIM + ROW, HEAD), F32)],
    )


def on_device(
    queries,
    key_rows,
    value_rows,
    doc_lengths,
    gate_input,
    bc_input,
    step_size,
    decay_rate,
    skip_gain,
    conv_x,
    conv_bc,
    norm_gain,
):
    ctx = lax.axis_index("ctx")
    tp = lax.axis_index("tp")
    near = ctx % NEAR
    core = tp % 2
    group = tp // 2
    place = jnp.stack([(ctx // NEAR) * ROW, near, core, ctx * SHARD]).astype(jnp.int32)
    info = jnp.concatenate([place, doc_lengths])
    rates = jnp.concatenate([decay_rate, skip_gain])

    bc_mine = lax.dynamic_slice(bc_input, (0, core, group, 0), (SHARD, 1, 1, STATE)).reshape(
        SHARD, STATE
    )
    taps_mine = lax.dynamic_slice(conv_bc, (0, core, group, 0), (4, 1, 1, STATE)).reshape(4, STATE)
    rim = from_shard_behind(jnp.concatenate([queries[SHARD - RIM :], bc_mine[SHARD - RIM :]], 1))
    wide = (NEAR, SHARD, 2 * HEAD)
    pairs = jnp.where(
        lax.broadcasted_iota(jnp.int32, wide, 2) < HEAD,
        jnp.broadcast_to(jnp.pad(key_rows, ((0, 0), (0, HEAD))), wide),
        jnp.broadcast_to(jnp.pad(value_rows, ((0, 0), (HEAD, 0))), wide),
    )
    side = from_row_behind(jnp.concatenate([key_rows[:SIDE], value_rows[:SIDE]], 0), 2)
    own = exchange_near(pairs.reshape(ROW, 2 * HEAD))
    seen = call(places_kernel, [((ROW, HEAD), F32)], (info,), smem=1)
    packed = call(
        pack_kernel,
        [((NEAR, PACK_ROWS, HEAD), BF16)],
        (info, queries, step_size, bc_mine, rim, taps_mine, side),
        smem=1,
        scratch=[pltpu.VMEM((RIM + SHARD, STATE), F32)],
    )
    own, packed = lax.optimization_barrier((own, packed))
    half = ROW // 2
    back1 = from_row_behind(own, 1)
    back2 = from_row_behind(own.reshape(NEAR, SHARD, 2 * HEAD)[:, SIDE:], 2)
    back3 = from_row_behind(own[half:], 3)
    received = exchange_near(packed.reshape(NEAR * PACK_ROWS, HEAD)).reshape(
        NEAR, PACK_ROWS, HEAD
    )
    weigh, decays, *own_part = call(
        ahead_kernel,
        [((ROW, HEAD), F32), ((16, STATE), F32)] + [((ROW, HEAD), F32)] * 3,
        (info, rates, received, own, seen),
        smem=2,
        mib=7,
    )
    received, weigh, back1, back2, back3, *own_part = lax.optimization_barrier(
        (received, weigh, back1, back2, back3, *own_part)
    )
    other = with_partner(received[:, BC_AT:SIDE_AT])
    attended = run_attend(info, received, back1, back2, back3, seen, *own_part)
    x, handed = run_scan(info, attended, received, other, conv_x, weigh, decays, seen)
    handed = lax.all_to_all(
        handed.reshape(FAR * (HEAD + 16), STATE),
        "ctx",
        0,
        0,
        axis_index_groups=far_groups(),
        tiled=True,
    ).reshape(FAR, HEAD + 16, STATE)
    y_inner, enter_row, c_row = call(
        inner_kernel,
        [((ROW, HEAD), F32), ((ROW, HEAD), F32), ((ROW, STATE), BF16)],
        (info, rates, received, other, x),
        smem=2,
        flops=1 << 30,
    )
    y_row = call(
        carried_kernel,
        [((ROW, HEAD), BF16)],
        (info, y_inner, enter_row, c_row, handed),
        smem=1,
    )
    y_heads = exchange_near(y_row).reshape(NEAR, SHARD, HEAD)
    sums = call(square_kernel, [((SHARD, HEAD), F32)], (y_heads, gate_input))
    partner = with_partner(sums)
    return call(
        norm_kernel,
        [((SHARD, NEAR * HEAD), BF16)],
        (y_heads, gate_input, sums, partner, norm_gain.reshape(1, -1)),
    )


def solution(mesh):
    return jax.shard_map(
        on_device,
        mesh=mesh,
        in_specs=(
            P("ctx", "tp"),
            P("ctx", "tp"),
            P("ctx", "tp"),
            P(),
            P("ctx", "tp"),
            P("ctx", None, None, None),
            P("ctx", "tp"),
            P("tp"),
            P("tp"),
            P(None, "tp"),
            P(),
            P("tp"),
        ),
        out_specs=P("ctx", "tp"),
        check_vma=False,
    )
```
